32 devices in a mesh: wide: 8 (over z, y), narrow: 4 (over x, core).
Axes of the slice: x: 2, y: 2, z: 4, core: 2. Of those that a mesh axis runs over, the one named last changes fastest.
Arguments:
- chemical_fractions: float32 [53, 16, 32, 128], P(None, 'wide', 'narrow'), may hold values from 0.1 to 1
- thermal_state: float32 [16, 32, 128], P('wide', 'narrow'), may hold values from 1 to 3
- ignited_stacks: int32 [16, 32], P('wide', 'narrow'), may hold values from 0 to 1, as said below
- spreading_number: float32 [53], replicated, may hold values from 0.02 to 0.15
- natural_exponent_scale: float32 [325], replicated, may hold values from -1 to 1
- arrhenius_energy: float32 [325], replicated, may hold values from 0.5 to 2
- incoming_stoichiometry: int32 [325, 53], replicated, may hold values 0 or 1
- outgoing_stoichiometry: int32 [325, 53], replicated, may hold values 0 or 1
Outputs:
- updated: float32 [53, 16, 32, 128], P(None, 'wide', 'narrow')
The draws below stay inside these ranges and needn't reach their ends.
Inputs may be any that keep to these rules, and one draw needn't show every extreme that they name: `ignited_stacks`: on each device either 8 or 2 of its columns burn. In every group of devices along narrow, those with 8 burning columns are a quarter of the group and consecutive in index, with wrap-around.
All inputs are finite; a program needn't handle non-finite values.
Results may differ from the reference program's by a relative error of at most 0.0001.
Values sent between devices are 32-bit elements; how exact they have to be, the bound alone decides.
A program may use at most 64 MiB of HBM per device.

```python
import math
import jax
import jax.numpy as jnp
from jax import lax

S = 53
R = 325
CX = 2
CY = 8
STACK_HEIGHT = 128
BURN_MAX = 8
MESH_LEADING = 16
MESH_TRAILING = 32
N_WIDE = 8
N_NARROW = 4


def draw_ignited_stacks(key, part):
    key_rank = jax.random.fold_in(key, 11)
    key_turn = jax.random.fold_in(key, 12)
    stack_total = CX * CY
    scores = jax.random.randint(key_rank, (N_WIDE, N_NARROW, stack_total), 0, 2 ** 20) * stack_total + jnp.arange(stack_total, dtype=jnp.int32)
    order = jnp.argsort(scores, axis=-1)
    ranks = jnp.argsort(order, axis=-1)
    turns = jax.random.randint(key_turn, (N_WIDE, 1), 0, N_NARROW)
    where_at = (jnp.arange(N_NARROW, dtype=jnp.int32)[None, :] + turns) % N_NARROW
    counts = jnp.where(where_at < N_NARROW // 4, BURN_MAX, BURN_MAX // 4)
    marks = (ranks < counts[:, :, None]).astype(jnp.int32)
    marks = marks.reshape(N_WIDE, N_NARROW, CX, CY)
    marks = jnp.transpose(marks, (0, 2, 1, 3))
    return marks.reshape(N_WIDE * CX, N_NARROW * CY)


def place_ends(array, key, least, high):
    shape = array.shape
    place = [jax.random.randint(jax.random.fold_in(key, axis), (), 0, shape[axis]) for axis in range(len(shape))]
    array = array.at[tuple(place)].set(least)
    longest = shape.index(max(shape))
    place[longest] = (place[longest] + 1) % shape[longest]
    return array.at[tuple(place)].set(high)


def shard_levels(stream_key, dims, pieces, least, high):
    level, own = 1.0, jax.random.fold_in(stream_key, 6)
    for axis_at, shards_of in pieces:
        draws = jnp.exp(jax.random.uniform(jax.random.fold_in(own, axis_at), (shards_of,), jnp.float32, least / len(pieces), high / len(pieces)))
        level = level * jnp.repeat(draws, dims[axis_at] // shards_of).reshape([-1 if axis == axis_at else 1 for axis in range(len(dims))])
    return level


def setup_inputs(seed: int = 0) -> dict:
    streams_of = jax.random.split(jax.random.key(seed), 9)
    return {
        "chemical_fractions": jnp.clip(jnp.exp(math.log(1.0) - 2.3025851 * jax.random.uniform(streams_of[0], (S, MESH_LEADING, MESH_TRAILING, STACK_HEIGHT), jnp.float32) ** shard_levels(streams_of[0], (S, MESH_LEADING, MESH_TRAILING, STACK_HEIGHT), ((1, 8), (2, 4)), -0.2, 0.2)), 0.1, 1.0),
        "thermal_state": jnp.clip(1.0 + 2.0 * jax.random.uniform(streams_of[1], (MESH_LEADING, MESH_TRAILING, STACK_HEIGHT), jnp.float32) ** shard_levels(streams_of[1], (MESH_LEADING, MESH_TRAILING, STACK_HEIGHT), ((0, 8), (1, 4)), -0.2, 0.2), 1.0, 3.0),
        "ignited_stacks": draw_ignited_stacks(jax.random.fold_in(streams_of[8], 71), 0),
        "spreading_number": jnp.clip(jax.random.uniform(streams_of[3], (S,), jnp.float32, 0.02, 0.15), 0.02, 0.15),
        "natural_exponent_scale": jnp.clip(jax.random.uniform(streams_of[4], (R,), jnp.float32, -1.0, 1.0), -1.0, 1.0),
        "arrhenius_energy": jnp.clip(jax.random.uniform(streams_of[5], (R,), jnp.float32, 0.5, 2.0), 0.5, 2.0),
        "incoming_stoichiometry": place_ends((jax.random.randint(streams_of[6], (R, S), 0, 20) < 1).astype(jnp.int32), jax.random.fold_in(streams_of[6], 1), 0, 1),
        "outgoing_stoichiometry": place_ends((jax.random.randint(streams_of[7], (R, S), 0, 20) < 1).astype(jnp.int32), jax.random.fold_in(streams_of[7], 1), 0, 1),
    }


def diffuse(fields, coeff):
    beside = jnp.roll(fields, -1, 1) + jnp.roll(fields, 1, 1)
    beside = beside + jnp.roll(fields, -1, 2) + jnp.roll(fields, 1, 2)
    beside = beside + jnp.roll(fields, -1, 3) + jnp.roll(fields, 1, 3)
    return fields + coeff * (beside - 6.0 * fields)


def react(values, enthalpy_output, natural_exponent_scale, arrhenius_energy, react_mat, react_tr, prod_tr):
    for substep in range(2):
        logs = jnp.log(values)
        expo = natural_exponent_scale[:, None] - arrhenius_energy[:, None] / enthalpy_output[None, :] + jnp.dot(react_mat, logs, precision=lax.Precision.HIGHEST, preferred_element_type=jnp.float32)
        rates = jnp.exp(expo)
        gain = jnp.dot(prod_tr, rates, precision=lax.Precision.HIGHEST, preferred_element_type=jnp.float32)
        loss = jnp.dot(react_tr, rates, precision=lax.Precision.HIGHEST, preferred_element_type=jnp.float32)
        values = values * (values + 0.5 * gain) / (values + 0.5 * loss)
    return values


def reference(chemical_fractions, thermal_state, ignited_stacks, spreading_number, natural_exponent_scale, arrhenius_energy, incoming_stoichiometry, outgoing_stoichiometry):
    coeff = spreading_number[:, None, None, None]
    fields = diffuse(diffuse(chemical_fractions, coeff), coeff)
    flat = fields.reshape(S, MESH_LEADING * MESH_TRAILING, STACK_HEIGHT)
    enthalpy_output = thermal_state.reshape(MESH_LEADING * MESH_TRAILING, STACK_HEIGHT)
    react_mat = incoming_stoichiometry.astype(jnp.float32)
    react_tr = react_mat.T
    prod_tr = outgoing_stoichiometry.astype(jnp.float32).T
    block_cols = 7 * BURN_MAX // 4
    total = N_WIDE * (N_NARROW // 4) * block_cols
    chosen = jnp.nonzero(ignited_stacks.reshape(-1), size=total)[0].astype(jnp.int32)
    blocks = chosen.reshape(-1, block_cols)

    def one_block(cols):
        picked = jnp.take(flat, cols, axis=1).reshape(S, -1)
        temps = jnp.take(enthalpy_output, cols, axis=0).reshape(-1)
        return react(picked, temps, natural_exponent_scale, arrhenius_energy, react_mat, react_tr, prod_tr).reshape(S, block_cols, STACK_HEIGHT)

    result = lax.map(one_block, blocks)
    result = jnp.transpose(result, (1, 0, 2, 3)).reshape(S, total, STACK_HEIGHT)
    flat = flat.at[:, chosen].set(result)
    return flat.reshape(S, MESH_LEADING, MESH_TRAILING, STACK_HEIGHT)
```

```python
import functools

import jax
import jax.numpy as jnp
from jax import lax
from jax.experimental import pallas as pl
from jax.experimental.pallas import tpu as pltpu
from jax.sharding import PartitionSpec as P

BURN_MAX = 8
CHUNKS = 4
MESH = pl.DeviceIdType.MESH


def pieces(total, count):
    edges = [total * i // count for i in range(count + 1)]
    return [(lo, hi - lo) for lo, hi in zip(edges[:-1], edges[1:])]


def in_plane(centre, up_edge, down_edge, row, coeff):
    last = centre.shape[1] - 1
    beside = jnp.where(row == 0, up_edge, pltpu.roll(centre, 1, 1))
    beside = beside + jnp.where(row == last, down_edge, pltpu.roll(centre, last, 1))
    beside = beside + pltpu.roll(centre, 1, 2) + pltpu.roll(centre, centre.shape[2] - 1, 2)
    return centre + coeff * (beside - 6.0 * centre)


def rolled(tile):
    return pltpu.roll(tile, 1, 1), pltpu.roll(tile, tile.shape[1] - 1, 1)


def exchange(
    n_wide, n_narrow, x_ref, c_ref, out_ref, xv, raw, corner_s, corner_r, halo_s, halo_r,
    sums_s, sums_r, local_sem, raw_ss, raw_rs, sums_ss, sums_rs, side_ss, side_rs,
):
    w, n = lax.axis_index("wide"), lax.axis_index("narrow")
    odd = w % 2
    near, far = 1 - odd, odd
    partner = w + 1 - 2 * odd
    target = (w + n_wide + 4 * odd - 2) % n_wide
    source = (w + n_wide + 2 - 4 * odd) % n_wide
    left, right = (n + n_narrow - 1) % n_narrow, (n + 1) % n_narrow
    nspec, _, cy, _ = xv.shape
    half = cy // 2
    chunks = pieces(nspec, CHUNKS)

    load = pltpu.make_async_copy(x_ref, xv, local_sem)
    load.start()
    barrier = pltpu.get_barrier_semaphore()
    for device in (
        (source, n), (source, left), (source, right), (w, left), (w, right), (partner, n)
    ):
        pl.semaphore_signal(barrier, inc=1, device_id=device, device_id_type=MESH)
    load.wait()
    corner_s[0] = xv[:, far, cy - 1, :]
    corner_s[1] = xv[:, far, 0, :]
    for start, size in chunks:
        sl = pl.ds(start, size)
        row = lax.broadcasted_iota(jnp.int32, (size,) + xv.shape[2:], 1)
        first, second = xv[sl, 0], pltpu.roll(xv[sl, 1], half, 1)
        halo_s[0, sl] = jnp.where(row >= half, first, second)
        halo_s[1, sl] = jnp.where(row < half, first, second)
    pl.semaphore_wait(barrier, 6)

    def send(src, dst, ss, rs, device):
        copy = pltpu.make_async_remote_copy(
            src_ref=src, dst_ref=dst, send_sem=ss, recv_sem=rs,
            device_id=device, device_id_type=MESH,
        )
        copy.start()
        return copy

    sides = [
        send(corner_s.at[0], corner_r.at[0], side_ss.at[0], side_rs.at[0], (target, right)),
        send(corner_s.at[1], corner_r.at[1], side_ss.at[1], side_rs.at[1], (target, left)),
        send(halo_s.at[0], halo_r.at[0], side_ss.at[2], side_rs.at[2], (w, right)),
        send(halo_s.at[1], halo_r.at[1], side_ss.at[3], side_rs.at[3], (w, left)),
    ]
    raws = []
    for k, (start, size) in enumerate(chunks):
        sl = pl.ds(start, size)
        raws.append(send(xv.at[sl], raw.at[sl], raw_ss.at[k], raw_rs.at[k], (target, n)))
    for copy in sides:
        copy.wait_recv()

    sums = []
    for k, (start, size) in enumerate(chunks):
        sl = pl.ds(start, size)
        coeff = c_ref[sl]
        square = coeff * coeff
        row = lax.broadcasted_iota(jnp.int32, (size,) + xv.shape[2:], 1)
        low, high = halo_r[0, sl], halo_r[1, sl]
        halos = (
            jnp.where(row < half, high, low),
            pltpu.roll(jnp.where(row < half, low, high), half, 1),
        )
        own_near, own_far = xv[sl, near], xv[sl, far]
        halo_near = jnp.where(near == 0, halos[0], halos[1])
        beyond = square * own_far + (2.0 * coeff) * in_plane(
            own_near, *rolled(halo_near), row, coeff
        )
        within = square * own_near
        raws[k].wait_recv()
        raw_near, raw_far = raw[sl, far], raw[sl, near]
        plane = in_plane(
            raw_near, corner_r[0, sl][:, None, :], corner_r[1, sl][:, None, :], row, coeff
        )
        sums_s[sl, near] = within + square * raw_far + (2.0 * coeff) * plane
        sums_s[sl, far] = beyond + square * raw_near
        sums.append(
            send(sums_s.at[sl], sums_r.at[sl], sums_ss.at[k], sums_rs.at[k], (partner, n))
        )
        for i in range(2):
            mine, other = xv[sl, i], xv[sl, 1 - i]
            centre = in_plane(mine, *rolled(halos[i]), row, coeff) + (2.0 * coeff) * other
            edge = in_plane(halos[i], *rolled(mine), row, coeff) + (2.0 * coeff) * halos[1 - i]
            out_ref[sl, i] = in_plane(centre, *rolled(edge), row, coeff) + (2.0 * square) * mine

    for k, (start, size) in enumerate(chunks):
        sl = pl.ds(start, size)
        sums[k].wait_recv()
        out_ref[sl] = out_ref[sl] + sums_r[sl]
    for copy in sides + raws + sums:
        copy.wait_send()


def two_parts(values):
    high = values.astype(jnp.bfloat16)
    return high, (values - high.astype(jnp.float32)).astype(jnp.bfloat16)


def reaction(
    marks_ref, mixed_ref, heat_ref, scale_ref, energy_ref, logs_ref, sums_ref, out_ref,
    picked, temps, stacked, slots,
):
    nspec = mixed_ref.shape[0] // heat_ref.shape[0]
    stacks, height = heat_ref.shape
    per_row = marks_ref.shape[1]
    room = stacked.shape[0] // 2
    pad = sums_ref.shape[0] // 2
    out_ref[...] = mixed_ref[...]
    for k in range(BURN_MAX):
        slots[k] = 0
    count = jnp.int32(0)
    for i in range(stacks):
        burning = marks_ref[i // per_row, i % per_row]

        @pl.when((burning == 1) & (count < BURN_MAX))
        def _():
            slots[count] = i

        count = count + burning
    for k in range(BURN_MAX):
        cells = pl.ds(k * height, height)
        picked[:, cells] = mixed_ref[pl.ds(slots[k], nspec, stride=stacks), :]
        temps[:, cells] = heat_ref[pl.ds(slots[k], 1), :]
    stacked[...] = jnp.zeros_like(stacked)
    base = scale_ref[...] - energy_ref[...] * (1.0 / temps[...])
    values = picked[...]
    for substep in range(2):
        high, low = two_parts(jnp.log(values))
        stacked[0:nspec, :] = high
        stacked[room : room + nspec, :] = low
        expo = base + jnp.dot(logs_ref[...], stacked[...], preferred_element_type=jnp.float32)
        high, low = two_parts(jnp.exp(expo))
        total = jnp.dot(sums_ref[...], high, preferred_element_type=jnp.float32)
        total = total + jnp.dot(sums_ref[...], low, preferred_element_type=jnp.float32)
        gain, loss = total[0:nspec], total[pad : pad + nspec]
        values = values * (values + 0.5 * gain) / (values + 0.5 * loss)
    picked[...] = values
    for k in range(BURN_MAX):

        @pl.when(k < count)
        def _():
            column = picked[:, k * height : (k + 1) * height]
            out_ref[pl.ds(slots[k], nspec, stride=stacks), :] = column


def round_up(value, step):
    return -(-value // step) * step


def shards(
    n_wide,
    n_narrow,
    chemical_fractions,
    thermal_state,
    ignited_stacks,
    spreading_number,
    natural_exponent_scale,
    arrhenius_energy,
    incoming_stoichiometry,
    outgoing_stoichiometry,
):
    shape = chemical_fractions.shape
    nspec, cx, cy, height = shape
    nreact = incoming_stoichiometry.shape[0]
    f32, bf16 = jnp.float32, jnp.bfloat16
    vmem = pl.BlockSpec(memory_space=pltpu.VMEM)
    smem = pl.BlockSpec(memory_space=pltpu.SMEM)
    coeff = jnp.broadcast_to(spreading_number[:, None, None], (nspec, 1, height))
    dma = pltpu.SemaphoreType.DMA
    mixed = pl.pallas_call(
        functools.partial(exchange, n_wide, n_narrow),
        out_shape=jax.ShapeDtypeStruct(shape, f32),
        in_specs=[pl.BlockSpec(memory_space=pl.ANY), vmem],
        out_specs=vmem,
        scratch_shapes=[
            pltpu.VMEM(shape, f32),
            pltpu.VMEM(shape, f32),
            pltpu.VMEM((2, nspec, height), f32),
            pltpu.VMEM((2, nspec, height), f32),
            pltpu.VMEM((2, nspec, cy, height), f32),
            pltpu.VMEM((2, nspec, cy, height), f32),
            pltpu.VMEM(shape, f32),
            pltpu.VMEM(shape, f32),
            dma(()),
            dma((CHUNKS,)),
            dma((CHUNKS,)),
            dma((CHUNKS,)),
            dma((CHUNKS,)),
            dma((4,)),
            dma((4,)),
        ],
        compiler_params=pltpu.CompilerParams(
            collective_id=0, has_side_effects=True, vmem_limit_bytes=32 * 2**20
        ),
        name="exchange",
    )(chemical_fractions, coeff)

    room, rows = round_up(nspec, 64), round_up(nreact, 16)
    pad = round_up(nspec, 8)
    more = rows - nreact
    incoming = jnp.pad(incoming_stoichiometry.astype(bf16), ((0, more), (0, 0)))
    outgoing = jnp.pad(outgoing_stoichiometry.astype(bf16), ((0, more), (0, 0)))
    logs_mat = jnp.tile(jnp.pad(incoming, ((0, 0), (0, room - nspec))), (1, 2))
    sums_mat = jnp.concatenate(
        [jnp.pad(m, ((0, 0), (0, pad - nspec))) for m in (outgoing, incoming)], axis=1
    ).T
    cells = BURN_MAX * height
    updated = pl.pallas_call(
        reaction,
        out_shape=jax.ShapeDtypeStruct((nspec * cx * cy, height), f32),
        in_specs=[smem] + [vmem] * 6,
        out_specs=vmem,
        scratch_shapes=[
            pltpu.VMEM((nspec, cells), f32),
            pltpu.VMEM((1, cells), f32),
            pltpu.VMEM((2 * room, cells), bf16),
            pltpu.SMEM((BURN_MAX,), jnp.int32),
        ],
        compiler_params=pltpu.CompilerParams(vmem_limit_bytes=32 * 2**20),
        name="reaction",
    )(
        ignited_stacks,
        mixed.reshape(nspec * cx * cy, height),
        thermal_state.reshape(cx * cy, height),
        jnp.pad(natural_exponent_scale, (0, more))[:, None],
        jnp.pad(arrhenius_energy, (0, more))[:, None],
        logs_mat,
        sums_mat,
    )
    return updated.reshape(shape)


def solution(mesh):
    in_specs = (
        P(None, "wide", "narrow", None),
        P("wide", "narrow", None),
        P("wide", "narrow"),
        P(),
        P(),
        P(),
        P(),
        P(),
    )
    out_specs = P(None, "wide", "narrow", None)
    body = functools.partial(shards, mesh.shape["wide"], mesh.shape["narrow"])
    return jax.shard_map(body, mesh=mesh, in_specs=in_specs, out_specs=out_specs, check_vma=False)
```

```python
import functools

import jax
import jax.numpy as jnp
from jax import lax
from jax.experimental import pallas as pl
from jax.experimental.pallas import tpu as pltpu
from jax.sharding import PartitionSpec as P

BURN_MAX = 8
CHUNKS = 8
MESH = pl.DeviceIdType.MESH


def pieces(total, count):
    edges = [total * i // count for i in range(count + 1)]
    return [(lo, hi - lo) for lo, hi in zip(edges[:-1], edges[1:])]


def in_plane(centre, up_edge, down_edge, row, coeff):
    last = centre.shape[1] - 1
    beside = jnp.where(row == 0, up_edge, pltpu.roll(centre, 1, 1))
    beside = beside + jnp.where(row == last, down_edge, pltpu.roll(centre, last, 1))
    beside = beside + pltpu.roll(centre, 1, 2) + pltpu.roll(centre, centre.shape[2] - 1, 2)
    return centre + coeff * (beside - 6.0 * centre)


def rolled(tile):
    return pltpu.roll(tile, 1, 1), pltpu.roll(tile, tile.shape[1] - 1, 1)


def exchange(
    n_wide, n_narrow, x_ref, c_ref, out_ref, xv, raw, corner_s, corner_r, edge_s, edge_r,
    rest_s, rest_r, sums_s, sums_r, local_sem, raw_ss, raw_rs, sums_ss, sums_rs,
    side_ss, side_rs,
):
    w, n = lax.axis_index("wide"), lax.axis_index("narrow")
    odd = w % 2
    near, far = 1 - odd, odd
    partner = w + 1 - 2 * odd
    target = (w + n_wide + 4 * odd - 2) % n_wide
    source = (w + n_wide + 2 - 4 * odd) % n_wide
    left, right = (n + n_narrow - 1) % n_narrow, (n + 1) % n_narrow
    nspec, _, cy, _ = xv.shape
    chunks = pieces(nspec, CHUNKS)

    load = pltpu.make_async_copy(x_ref, xv, local_sem)
    load.start()
    barrier = pltpu.get_barrier_semaphore()
    for device in (
        (source, n), (source, left), (source, right), (w, left), (w, right), (partner, n)
    ):
        pl.semaphore_signal(barrier, inc=1, device_id=device, device_id_type=MESH)
    load.wait()
    for side, (row, inner) in enumerate(((cy - 1, cy - 2), (0, 1))):
        corner_s[side] = xv[:, far, row, :]
        edge_s[side] = xv[:, near, row, :]
        rest_s[side, 0] = xv[:, far, row, :]
        rest_s[side, 1] = xv[:, near, inner, :]
        rest_s[side, 2] = xv[:, far, inner, :]
    pl.semaphore_wait(barrier, 6)

    def send(src, dst, ss, rs, device):
        copy = pltpu.make_async_remote_copy(
            src_ref=src, dst_ref=dst, send_sem=ss, recv_sem=rs,
            device_id=device, device_id_type=MESH,
        )
        copy.start()
        return copy

    raws, sums = [], []

    def send_raw(k):
        sl = pl.ds(*chunks[k])
        raws.append(send(xv.at[sl], raw.at[sl], raw_ss.at[k], raw_rs.at[k], (target, n)))

    send_raw(0)
    sides = []
    for side, to in enumerate((right, left)):
        for j, (src, dst, device) in enumerate((
            (corner_s, corner_r, (target, to)),
            (edge_s, edge_r, (w, to)),
        )):
            at = 2 * j + side
            sides.append(
                send(src.at[side], dst.at[side], side_ss.at[at], side_rs.at[at], device)
            )
    send_raw(1)
    rests = [
        send(rest_s.at[side], rest_r.at[side], side_ss.at[4 + side], side_rs.at[4 + side], (w, to))
        for side, to in enumerate((right, left))
    ]
    for copy in sides:
        copy.wait_recv()

    for k, (start, size) in enumerate(chunks):
        sl = pl.ds(start, size)
        coeff = c_ref[sl]
        square, twice = coeff * coeff, 2.0 * coeff
        row = lax.broadcasted_iota(jnp.int32, (size,) + xv.shape[2:], 1)
        low, high = edge_r[0, sl][:, None, :], edge_r[1, sl][:, None, :]
        own_near, own_far = xv[sl, near], xv[sl, far]
        plane = in_plane(own_near, low, high, row, coeff)
        raws[k].wait_recv()
        if k + 2 < len(chunks):
            send_raw(k + 2)
        raw_near, raw_far = raw[sl, far], raw[sl, near]
        sums_s[sl, far] = twice * plane + square * (own_far + raw_near)
        beyond = in_plane(
            raw_near, corner_r[0, sl][:, None, :], corner_r[1, sl][:, None, :], row, coeff
        )
        sums_s[sl, near] = twice * beyond + square * (own_near + raw_far)
        sums.append(
            send(sums_s.at[sl], sums_r.at[sl], sums_ss.at[k], sums_rs.at[k], (partner, n))
        )
        if k == 0:
            for copy in rests:
                copy.wait_recv()

        def halo(low, high, low_inner, high_inner):
            tile = jnp.where(row == 0, high, high_inner[:, None, :])
            return jnp.where(row == cy - 1, low, jnp.where(row == cy - 2, low_inner[:, None, :], tile))

        halo_near = halo(low, high, rest_r[0, 1, sl], rest_r[1, 1, sl])
        halo_far = halo(
            rest_r[0, 0, sl][:, None, :], rest_r[1, 0, sl][:, None, :],
            rest_r[0, 2, sl], rest_r[1, 2, sl],
        )
        for at, mine, other, side, across, flat in (
            (near, own_near, own_far, halo_near, halo_far, plane),
            (far, own_far, own_near, halo_far, halo_near, None),
        ):
            if flat is None:
                flat = in_plane(mine, *rolled(side), row, coeff)
            centre = flat + twice * other
            edge = in_plane(side, *rolled(mine), row, coeff) + twice * across
            out_ref[sl, at] = in_plane(centre, *rolled(edge), row, coeff) + 2.0 * square * mine

    for k, (start, size) in enumerate(chunks):
        sl = pl.ds(start, size)
        sums[k].wait_recv()
        out_ref[sl] = out_ref[sl] + sums_r[sl]
    for copy in sides + rests + raws + sums:
        copy.wait_send()


def two_parts(values):
    high = values.astype(jnp.bfloat16)
    return high, (values - high.astype(jnp.float32)).astype(jnp.bfloat16)


def reaction(
    marks_ref, mixed_ref, heat_ref, scale_ref, energy_ref, logs_ref, sums_ref, out_ref,
    picked, temps, stacked, slots,
):
    nspec = mixed_ref.shape[0] // heat_ref.shape[0]
    stacks, height = heat_ref.shape
    per_row = marks_ref.shape[1]
    room = stacked.shape[0] // 2
    pad = sums_ref.shape[0] // 2
    out_ref[...] = mixed_ref[...]
    for k in range(BURN_MAX):
        slots[k] = 0
    count = jnp.int32(0)
    for i in range(stacks):
        burning = marks_ref[i // per_row, i % per_row]

        @pl.when((burning == 1) & (count < BURN_MAX))
        def _():
            slots[count] = i

        count = count + burning
    for k in range(BURN_MAX):
        cells = pl.ds(k * height, height)
        picked[:, cells] = mixed_ref[pl.ds(slots[k], nspec, stride=stacks), :]
        temps[:, cells] = heat_ref[pl.ds(slots[k], 1), :]
    stacked[...] = jnp.zeros_like(stacked)
    base = scale_ref[...] - energy_ref[...] * (1.0 / temps[...])
    values = picked[...]
    for substep in range(2):
        high, low = two_parts(jnp.log(values))
        stacked[0:nspec, :] = high
        stacked[room : room + nspec, :] = low
        expo = base + jnp.dot(logs_ref[...], stacked[...], preferred_element_type=jnp.float32)
        high, low = two_parts(jnp.exp(expo))
        total = jnp.dot(sums_ref[...], high, preferred_element_type=jnp.float32)
        total = total + jnp.dot(sums_ref[...], low, preferred_element_type=jnp.float32)
        gain, loss = total[0:nspec], total[pad : pad + nspec]
        values = values * (values + 0.5 * gain) / (values + 0.5 * loss)
    picked[...] = values
    for k in range(BURN_MAX):

        @pl.when(k < count)
        def _():
            column = picked[:, k * height : (k + 1) * height]
            out_ref[pl.ds(slots[k], nspec, stride=stacks), :] = column


def round_up(value, step):
    return -(-value // step) * step


def shards(
    n_wide,
    n_narrow,
    chemical_fractions,
    thermal_state,
    ignited_stacks,
    spreading_number,
    natural_exponent_scale,
    arrhenius_energy,
    incoming_stoichiometry,
    outgoing_stoichiometry,
):
    shape = chemical_fractions.shape
    nspec, cx, cy, height = shape
    nreact = incoming_stoichiometry.shape[0]
    f32, bf16 = jnp.float32, jnp.bfloat16
    vmem = pl.BlockSpec(memory_space=pltpu.VMEM)
    smem = pl.BlockSpec(memory_space=pltpu.SMEM)
    coeff = jnp.broadcast_to(spreading_number[:, None, None], (nspec, 1, height))
    dma = pltpu.SemaphoreType.DMA
    mixed = pl.pallas_call(
        functools.partial(exchange, n_wide, n_narrow),
        out_shape=jax.ShapeDtypeStruct(shape, f32),
        in_specs=[pl.BlockSpec(memory_space=pl.ANY), vmem],
        out_specs=vmem,
        scratch_shapes=[
            pltpu.VMEM(shape, f32),
            pltpu.VMEM(shape, f32),
            pltpu.VMEM((2, nspec, height), f32),
            pltpu.VMEM((2, nspec, height), f32),
            pltpu.VMEM((2, nspec, height), f32),
            pltpu.VMEM((2, nspec, height), f32),
            pltpu.VMEM((2, 3, nspec, height), f32),
            pltpu.VMEM((2, 3, nspec, height), f32),
            pltpu.VMEM(shape, f32),
            pltpu.VMEM(shape, f32),
            dma(()),
            dma((CHUNKS,)),
            dma((CHUNKS,)),
            dma((CHUNKS,)),
            dma((CHUNKS,)),
            dma((6,)),
            dma((6,)),
        ],
        compiler_params=pltpu.CompilerParams(
            collective_id=0, has_side_effects=True, vmem_limit_bytes=32 * 2**20
        ),
        name="exchange",
    )(chemical_fractions, coeff)

    room, rows = round_up(nspec, 64), round_up(nreact, 16)
    pad = round_up(nspec, 8)
    more = rows - nreact
    incoming = jnp.pad(incoming_stoichiometry.astype(bf16), ((0, more), (0, 0)))
    outgoing = jnp.pad(outgoing_stoichiometry.astype(bf16), ((0, more), (0, 0)))
    logs_mat = jnp.tile(jnp.pad(incoming, ((0, 0), (0, room - nspec))), (1, 2))
    sums_mat = jnp.concatenate(
        [jnp.pad(m, ((0, 0), (0, pad - nspec))) for m in (outgoing, incoming)], axis=1
    ).T
    cells = BURN_MAX * height
    updated = pl.pallas_call(
        reaction,
        out_shape=jax.ShapeDtypeStruct((nspec * cx * cy, height), f32),
        in_specs=[smem] + [vmem] * 6,
        out_specs=vmem,
        scratch_shapes=[
            pltpu.VMEM((nspec, cells), f32),
            pltpu.VMEM((1, cells), f32),
            pltpu.VMEM((2 * room, cells), bf16),
            pltpu.SMEM((BURN_MAX,), jnp.int32),
        ],
        compiler_params=pltpu.CompilerParams(vmem_limit_bytes=32 * 2**20),
        name="reaction",
    )(
        ignited_stacks,
        mixed.reshape(nspec * cx * cy, height),
        thermal_state.reshape(cx * cy, height),
        jnp.pad(natural_exponent_scale, (0, more))[:, None],
        jnp.pad(arrhenius_energy, (0, more))[:, None],
        logs_mat,
        sums_mat,
    )
    return updated.reshape(shape)


def solution(mesh):
    in_specs = (
        P(None, "wide", "narrow", None),
        P("wide", "narrow", None),
        P("wide", "narrow"),
        P(),
        P(),
        P(),
        P(),
        P(),
    )
    out_specs = P(None, "wide", "narrow", None)
    body = functools.partial(shards, mesh.shape["wide"], mesh.shape["narrow"])
    return jax.shard_map(body, mesh=mesh, in_specs=in_specs, out_specs=out_specs, check_vma=False)
```

```python
import functools

import jax
import jax.numpy as jnp
from jax import lax
from jax.experimental import pallas as pl
from jax.experimental.pallas import tpu as pltpu
from jax.sharding import PartitionSpec as P

BURN_MAX = 8
EARLY = 3
LATE = 3
MESH = pl.DeviceIdType.MESH


def pieces(total, count):
    edges = [total * i // count for i in range(count + 1)]
    return [(lo, hi - lo) for lo, hi in zip(edges[:-1], edges[1:])]


def in_plane(centre, up_edge, down_edge, row, coeff):
    last = centre.shape[1] - 1
    beside = jnp.where(row == 0, up_edge, pltpu.roll(centre, 1, 1))
    beside = beside + jnp.where(row == last, down_edge, pltpu.roll(centre, last, 1))
    beside = beside + pltpu.roll(centre, 1, 2) + pltpu.roll(centre, centre.shape[2] - 1, 2)
    return centre + coeff * (beside - 6.0 * centre)


def rolled(tile):
    return pltpu.roll(tile, 1, 1), pltpu.roll(tile, tile.shape[1] - 1, 1)


def exchange(
    n_wide, n_narrow, x_ref, c_ref, out_ref, xv, raw, sums_s, sums_r, part, beyond,
    corner_s, corner_r, touch_s, touch_r, edge_s, edge_r, rest_s, rest_r, local_sem,
    raw_ss, raw_rs, sums_ss, sums_rs, part_ss, part_rs, pass_ss, pass_rs, side_ss, side_rs,
):
    w, n = lax.axis_index("wide"), lax.axis_index("narrow")
    odd = w % 2
    near, far = 1 - odd, odd
    partner = w + 1 - 2 * odd
    other = (w + n_wide + 2 * odd - 1) % n_wide
    target = (w + n_wide + 4 * odd - 2) % n_wide
    source = (w + n_wide + 2 - 4 * odd) % n_wide
    left, right = (n + n_narrow - 1) % n_narrow, (n + 1) % n_narrow
    nspec, _, cy, _ = xv.shape
    early, late = raw.shape[0], part.shape[0]
    early_chunks, late_chunks = pieces(early, EARLY), pieces(late, LATE)

    load = pltpu.make_async_copy(x_ref, xv, local_sem)
    load.start()
    barrier = pltpu.get_barrier_semaphore()
    greeted = [(w, left), (w, right)]
    greeted += [(a, b) for a in (source, partner) for b in (n, left, right)]
    greeted += [(other, left), (other, right), (target, n)]
    for device in greeted:
        pl.semaphore_signal(barrier, inc=1, device_id=device, device_id_type=MESH)
    load.wait()
    for side, (row, inner) in enumerate(((cy - 1, cy - 2), (0, 1))):
        corner_s[side] = xv[0:early, far, row, :]
        touch_s[side, 0] = xv[early:nspec, near, row, :]
        touch_s[side, 1] = xv[early:nspec, far, row, :]
        edge_s[side] = xv[:, near, row, :]
        rest_s[side, 0] = xv[:, far, row, :]
        rest_s[side, 1] = xv[:, near, inner, :]
        rest_s[side, 2] = xv[:, far, inner, :]
    pl.semaphore_wait(barrier, len(greeted))

    def send(src, dst, ss, rs, device):
        copy = pltpu.make_async_remote_copy(
            src_ref=src, dst_ref=dst, send_sem=ss, recv_sem=rs,
            device_id=device, device_id_type=MESH,
        )
        copy.start()
        return copy

    def sides_of(at, src, dst, row):
        return [
            send(src(side), dst(side), side_ss.at[at + side], side_rs.at[at + side], (row, to))
            for side, to in enumerate((right, left))
        ]

    corners = sides_of(0, lambda i: corner_s.at[i], lambda i: corner_r.at[i], target)
    edges = sides_of(2, lambda i: edge_s.at[i], lambda i: edge_r.at[i], w)
    raws, parts = [], []
    for k in range(max(EARLY, LATE)):
        if k < EARLY:
            sl = pl.ds(*early_chunks[k])
            raws.append(send(xv.at[sl], raw.at[sl], raw_ss.at[k], raw_rs.at[k], (target, n)))
        if k < LATE:
            start, size = late_chunks[k]
            parts.append(
                send(
                    xv.at[pl.ds(early + start, size)], part.at[pl.ds(start, size)],
                    part_ss.at[k], part_rs.at[k], (partner, n),
                )
            )
    rests = sides_of(4, lambda i: rest_s.at[i], lambda i: rest_r.at[i], w)
    touches = sides_of(6, lambda i: touch_s.at[i, 0], lambda i: touch_r.at[i, 0], partner)
    touches += sides_of(8, lambda i: touch_s.at[i, 1], lambda i: touch_r.at[i, 1], other)
    for copy in corners + edges:
        copy.wait_recv()

    def rows_of(size):
        return lax.broadcasted_iota(jnp.int32, (size,) + xv.shape[2:], 1)

    sums, passes = [], []
    for k in range(max(EARLY, LATE)):
        if k < LATE:
            sl = pl.ds(*late_chunks[k])
            parts[k].wait_recv()
            passes.append(
                send(part.at[sl], beyond.at[sl], pass_ss.at[k], pass_rs.at[k], (source, n))
            )
        if k < EARLY:
            start, size = early_chunks[k]
            sl, row = pl.ds(start, size), rows_of(size)
            coeff = c_ref[sl]
            square, twice = coeff * coeff, 2.0 * coeff
            own_near, own_far = xv[sl, near], xv[sl, far]
            plane = in_plane(
                own_near, edge_r[0, sl][:, None, :], edge_r[1, sl][:, None, :], row, coeff
            )
            raws[k].wait_recv()
            raw_near, raw_far = raw[sl, far], raw[sl, near]
            sums_s[sl, far] = twice * plane + square * (own_far + raw_near)
            plane = in_plane(
                raw_near, corner_r[0, sl][:, None, :], corner_r[1, sl][:, None, :], row, coeff
            )
            sums_s[sl, near] = twice * plane + square * (own_near + raw_far)
            sums.append(
                send(sums_s.at[sl], sums_r.at[sl], sums_ss.at[k], sums_rs.at[k], (partner, n))
            )

    for copy in rests:
        copy.wait_recv()
    for start, size in pieces(nspec, EARLY + LATE):
        sl, row = pl.ds(start, size), rows_of(size)
        coeff = c_ref[sl]
        square, twice = coeff * coeff, 2.0 * coeff

        def halo(low, high, low_inner, high_inner):
            low, high, low_inner, high_inner = (
                v[:, None, :] for v in (low, high, low_inner, high_inner)
            )
            tile = jnp.where(row == 0, high, high_inner)
            return jnp.where(row == cy - 1, low, jnp.where(row == cy - 2, low_inner, tile))

        own = xv[sl, near], xv[sl, far]
        halos = (
            halo(edge_r[0, sl], edge_r[1, sl], rest_r[0, 1, sl], rest_r[1, 1, sl]),
            halo(rest_r[0, 0, sl], rest_r[1, 0, sl], rest_r[0, 2, sl], rest_r[1, 2, sl]),
        )
        for i, at in enumerate((near, far)):
            mine, side = own[i], halos[i]
            centre = in_plane(mine, *rolled(side), row, coeff) + twice * own[1 - i]
            edge = in_plane(side, *rolled(mine), row, coeff) + twice * halos[1 - i]
            out_ref[sl, at] = in_plane(centre, *rolled(edge), row, coeff) + 2.0 * square * mine

    for copy in touches:
        copy.wait_recv()
    for k in range(max(EARLY, LATE)):
        if k < EARLY:
            sl = pl.ds(*early_chunks[k])
            sums[k].wait_recv()
            out_ref[sl] = out_ref[sl] + sums_r[sl]
        if k < LATE:
            start, size = late_chunks[k]
            sl, to, row = pl.ds(start, size), pl.ds(early + start, size), rows_of(size)
            coeff = c_ref[to]
            square, twice = coeff * coeff, 2.0 * coeff
            close, second = part[sl, far], part[sl, near]
            plane = twice * in_plane(
                close, touch_r[0, 0, sl][:, None, :], touch_r[1, 0, sl][:, None, :], row, coeff
            )
            passes[k].wait_recv()
            ahead, third = beyond[sl, near], beyond[sl, far]
            out_ref[to, near] = out_ref[to, near] + plane + square * (second + ahead)
            plane = twice * in_plane(
                ahead, touch_r[0, 1, sl][:, None, :], touch_r[1, 1, sl][:, None, :], row, coeff
            )
            out_ref[to, far] = out_ref[to, far] + plane + square * (third + close)
    for copy in corners + edges + rests + touches + raws + parts + sums + passes:
        copy.wait_send()


def two_parts(values):
    high = values.astype(jnp.bfloat16)
    return high, (values - high.astype(jnp.float32)).astype(jnp.bfloat16)


def reaction(
    marks_ref, mixed_ref, heat_ref, scale_ref, energy_ref, logs_ref, sums_ref, out_ref,
    picked, temps, stacked, slots,
):
    nspec = mixed_ref.shape[0] // heat_ref.shape[0]
    stacks, height = heat_ref.shape
    per_row = marks_ref.shape[1]
    room = stacked.shape[0] // 2
    pad = sums_ref.shape[0] // 2
    out_ref[...] = mixed_ref[...]
    for k in range(BURN_MAX):
        slots[k] = 0
    count = jnp.int32(0)
    for i in range(stacks):
        burning = marks_ref[i // per_row, i % per_row]

        @pl.when((burning == 1) & (count < BURN_MAX))
        def _():
            slots[count] = i

        count = count + burning
    for k in range(BURN_MAX):
        cells = pl.ds(k * height, height)
        picked[:, cells] = mixed_ref[pl.ds(slots[k], nspec, stride=stacks), :]
        temps[:, cells] = heat_ref[pl.ds(slots[k], 1), :]
    stacked[...] = jnp.zeros_like(stacked)
    base = scale_ref[...] - energy_ref[...] * (1.0 / temps[...])
    values = picked[...]
    for substep in range(2):
        high, low = two_parts(jnp.log(values))
        stacked[0:nspec, :] = high
        stacked[room : room + nspec, :] = low
        expo = base + jnp.dot(logs_ref[...], stacked[...], preferred_element_type=jnp.float32)
        high, low = two_parts(jnp.exp(expo))
        total = jnp.dot(sums_ref[...], high, preferred_element_type=jnp.float32)
        total = total + jnp.dot(sums_ref[...], low, preferred_element_type=jnp.float32)
        gain, loss = total[0:nspec], total[pad : pad + nspec]
        values = values * (values + 0.5 * gain) / (values + 0.5 * loss)
    picked[...] = values
    for k in range(BURN_MAX):

        @pl.when(k < count)
        def _():
            column = picked[:, k * height : (k + 1) * height]
            out_ref[pl.ds(slots[k], nspec, stride=stacks), :] = column


def round_up(value, step):
    return -(-value // step) * step


def shards(
    n_wide,
    n_narrow,
    chemical_fractions,
    thermal_state,
    ignited_stacks,
    spreading_number,
    natural_exponent_scale,
    arrhenius_energy,
    incoming_stoichiometry,
    outgoing_stoichiometry,
):
    shape = chemical_fractions.shape
    nspec, cx, cy, height = shape
    nreact = incoming_stoichiometry.shape[0]
    f32, bf16 = jnp.float32, jnp.bfloat16
    vmem = pl.BlockSpec(memory_space=pltpu.VMEM)
    smem = pl.BlockSpec(memory_space=pltpu.SMEM)
    coeff = jnp.broadcast_to(spreading_number[:, None, None], (nspec, 1, height))
    dma = pltpu.SemaphoreType.DMA
    early = nspec // 16 * 8
    mixed = pl.pallas_call(
        functools.partial(exchange, n_wide, n_narrow),
        out_shape=jax.ShapeDtypeStruct(shape, f32),
        in_specs=[pl.BlockSpec(memory_space=pl.ANY), vmem],
        out_specs=vmem,
        scratch_shapes=[
            pltpu.VMEM(shape, f32),
            *[pltpu.VMEM((early,) + shape[1:], f32)] * 3,
            *[pltpu.VMEM((nspec - early,) + shape[1:], f32)] * 2,
            *[pltpu.VMEM((2, early, height), f32)] * 2,
            *[pltpu.VMEM((2, 2, nspec - early, height), f32)] * 2,
            *[pltpu.VMEM((2, nspec, height), f32)] * 2,
            *[pltpu.VMEM((2, 3, nspec, height), f32)] * 2,
            dma(()),
            *[dma((EARLY,))] * 4,
            *[dma((LATE,))] * 4,
            *[dma((10,))] * 2,
        ],
        compiler_params=pltpu.CompilerParams(
            collective_id=0, has_side_effects=True, vmem_limit_bytes=32 * 2**20
        ),
        name="exchange",
    )(chemical_fractions, coeff)

    room, rows = round_up(nspec, 64), round_up(nreact, 16)
    pad = round_up(nspec, 8)
    more = rows - nreact
    incoming = jnp.pad(incoming_stoichiometry.astype(bf16), ((0, more), (0, 0)))
    outgoing = jnp.pad(outgoing_stoichiometry.astype(bf16), ((0, more), (0, 0)))
    logs_mat = jnp.tile(jnp.pad(incoming, ((0, 0), (0, room - nspec))), (1, 2))
    sums_mat = jnp.concatenate(
        [jnp.pad(m, ((0, 0), (0, pad - nspec))) for m in (outgoing, incoming)], axis=1
    ).T
    cells = BURN_MAX * height
    updated = pl.pallas_call(
        reaction,
        out_shape=jax.ShapeDtypeStruct((nspec * cx * cy, height), f32),
        in_specs=[smem] + [vmem] * 6,
        out_specs=vmem,
        scratch_shapes=[
            pltpu.VMEM((nspec, cells), f32),
            pltpu.VMEM((1, cells), f32),
            pltpu.VMEM((2 * room, cells), bf16),
            pltpu.SMEM((BURN_MAX,), jnp.int32),
        ],
        compiler_params=pltpu.CompilerParams(vmem_limit_bytes=32 * 2**20),
        name="reaction",
    )(
        ignited_stacks,
        mixed.reshape(nspec * cx * cy, height),
        thermal_state.reshape(cx * cy, height),
        jnp.pad(natural_exponent_scale, (0, more))[:, None],
        jnp.pad(arrhenius_energy, (0, more))[:, None],
        logs_mat,
        sums_mat,
    )
    return updated.reshape(shape)


def solution(mesh):
    in_specs = (
        P(None, "wide", "narrow", None),
        P("wide", "narrow", None),
        P("wide", "narrow"),
        P(),
        P(),
        P(),
        P(),
        P(),
    )
    out_specs = P(None, "wide", "narrow", None)
    body = functools.partial(shards, mesh.shape["wide"], mesh.shape["narrow"])
    return jax.shard_map(body, mesh=mesh, in_specs=in_specs, out_specs=out_specs, check_vma=False)
```

```python
import functools

import jax
import jax.numpy as jnp
from jax import lax
from jax.experimental import pallas as pl
from jax.experimental.pallas import tpu as pltpu
from jax.sharding import PartitionSpec as P

BURN_MAX = 8
EARLY = 3
LATE = 3
MESH = pl.DeviceIdType.MESH


def pieces(total, count):
    edges = [total * i // count for i in range(count + 1)]
    return [(lo, hi - lo) for lo, hi in zip(edges[:-1], edges[1:])]


def in_plane(centre, up_edge, down_edge, row, coeff):
    last = centre.shape[1] - 1
    beside = jnp.where(row == 0, up_edge, pltpu.roll(centre, 1, 1))
    beside = beside + jnp.where(row == last, down_edge, pltpu.roll(centre, last, 1))
    beside = beside + pltpu.roll(centre, 1, 2) + pltpu.roll(centre, centre.shape[2] - 1, 2)
    return centre + coeff * (beside - 6.0 * centre)


def rolled(tile):
    return pltpu.roll(tile, 1, 1), pltpu.roll(tile, tile.shape[1] - 1, 1)


def three_parts(values):
    parts = []
    for _ in range(3):
        parts.append(values.astype(jnp.bfloat16).astype(jnp.float32))
        values = values - parts[-1]
    return parts


def rows_by_index(shape, rows):
    index = lax.broadcasted_iota(jnp.int32, shape, 0)
    block = jnp.zeros(shape, jnp.float32)
    for i, row in enumerate(rows):
        block = jnp.where(index == i, row, block)
    return block


def prepare(scale_ref, energy_ref, incoming_ref, outgoing_ref, work, logs_ref, sums_ref):
    nspec, nreact = incoming_ref.shape
    room, pad = logs_ref.shape[1] // 4, sums_ref.shape[0] // 2
    rows = logs_ref.shape[0]
    incoming = incoming_ref[...].astype(jnp.float32)
    work[...] = jnp.zeros_like(work)
    work[0:nspec, 0:nreact] = outgoing_ref[...].astype(jnp.float32)
    work[pad : pad + nspec, 0:nreact] = incoming
    sums_ref[...] = work[0 : 2 * pad, 0:rows].astype(jnp.bfloat16)
    work[...] = jnp.zeros_like(work)
    work[0:nspec, 0:nreact] = incoming
    work[room : room + nspec, 0:nreact] = incoming
    a, e = three_parts(scale_ref[...][None]), three_parts(-energy_ref[...][None])
    extra = (a[0], a[1], a[2], e[0], e[0], e[1], e[1], e[0], e[2])
    work[2 * room : 2 * room + 16, 0:nreact] = rows_by_index((16, nreact), extra)
    logs_ref[...] = work[...].T[0:rows].astype(jnp.bfloat16)


def exchange(
    n_wide, n_narrow, x_ref, coeff_hbm, marks_hbm, scale_hbm, energy_hbm, incoming_hbm,
    outgoing_hbm, out_ref, marks_ref, logs_ref, sums_ref, coeff_ref, scale_ref, energy_ref,
    incoming_ref, outgoing_ref, work, c_ref, load_sem, xv, raw, sums_s, sums_r, part, beyond,
    corner_s, corner_r, touch_s, touch_r, edge_s, edge_r, rest_s, rest_r, local_sem,
    raw_ss, raw_rs, sums_ss, sums_rs, part_ss, part_rs, pass_ss, pass_rs, side_ss, side_rs,
):
    w, n = lax.axis_index("wide"), lax.axis_index("narrow")
    odd = w % 2
    near, far = 1 - odd, odd
    partner = w + 1 - 2 * odd
    other = (w + n_wide + 2 * odd - 1) % n_wide
    target = (w + n_wide + 4 * odd - 2) % n_wide
    source = (w + n_wide + 2 - 4 * odd) % n_wide
    left, right = (n + n_narrow - 1) % n_narrow, (n + 1) % n_narrow
    nspec, _, cy, _ = xv.shape
    early, late = raw.shape[0], part.shape[0]
    early_chunks, late_chunks = pieces(early, EARLY), pieces(late, LATE)

    load = pltpu.make_async_copy(x_ref, xv, local_sem)
    load.start()
    loads = [
        pltpu.make_async_copy(src, dst, load_sem.at[i])
        for i, (src, dst) in enumerate((
            (coeff_hbm, coeff_ref), (marks_hbm, marks_ref), (scale_hbm, scale_ref),
            (energy_hbm, energy_ref), (incoming_hbm, incoming_ref), (outgoing_hbm, outgoing_ref),
        ))
    ]
    for copy in loads:
        copy.start()
    barrier = pltpu.get_barrier_semaphore()
    greeted = [(w, left), (w, right)]
    greeted += [(a, b) for a in (source, partner) for b in (n, left, right)]
    greeted += [(other, left), (other, right), (target, n)]
    for device in greeted:
        pl.semaphore_signal(barrier, inc=1, device_id=device, device_id_type=MESH)
    load.wait()
    for side, (row, inner) in enumerate(((cy - 1, cy - 2), (0, 1))):
        corner_s[side] = xv[0:early, far, row, :]
        touch_s[side, 0] = xv[early:nspec, near, row, :]
        touch_s[side, 1] = xv[early:nspec, far, row, :]
        edge_s[side] = xv[:, near, row, :]
        rest_s[side, 0] = xv[:, far, row, :]
        rest_s[side, 1] = xv[:, near, inner, :]
        rest_s[side, 2] = xv[:, far, inner, :]
    pl.semaphore_wait(barrier, len(greeted))

    def send(src, dst, ss, rs, device):
        copy = pltpu.make_async_remote_copy(
            src_ref=src, dst_ref=dst, send_sem=ss, recv_sem=rs,
            device_id=device, device_id_type=MESH,
        )
        copy.start()
        return copy

    def sides_of(at, src, dst, row):
        return [
            send(src(side), dst(side), side_ss.at[at + side], side_rs.at[at + side], (row, to))
            for side, to in enumerate((right, left))
        ]

    corners = sides_of(0, lambda i: corner_s.at[i], lambda i: corner_r.at[i], target)
    edges = sides_of(2, lambda i: edge_s.at[i], lambda i: edge_r.at[i], w)
    raws, parts = [], []
    for k in range(max(EARLY, LATE)):
        if k < EARLY:
            sl = pl.ds(*early_chunks[k])
            raws.append(send(xv.at[sl], raw.at[sl], raw_ss.at[k], raw_rs.at[k], (target, n)))
        if k < LATE:
            start, size = late_chunks[k]
            parts.append(
                send(
                    xv.at[pl.ds(early + start, size)], part.at[pl.ds(start, size)],
                    part_ss.at[k], part_rs.at[k], (partner, n),
                )
            )
    rests = sides_of(4, lambda i: rest_s.at[i], lambda i: rest_r.at[i], w)
    touches = sides_of(6, lambda i: touch_s.at[i, 0], lambda i: touch_r.at[i, 0], partner)
    touches += sides_of(8, lambda i: touch_s.at[i, 1], lambda i: touch_r.at[i, 1], other)
    for copy in loads:
        copy.wait()
    for i in range(nspec):
        c_ref[i] = jnp.full(c_ref.shape[1:], coeff_ref[0, i], jnp.float32)
    prepare(scale_ref, energy_ref, incoming_ref, outgoing_ref, work, logs_ref, sums_ref)
    for copy in corners + edges:
        copy.wait_recv()

    def rows_of(size):
        return lax.broadcasted_iota(jnp.int32, (size,) + xv.shape[2:], 1)

    sums, passes = [], []
    for k in range(max(EARLY, LATE)):
        if k < LATE:
            sl = pl.ds(*late_chunks[k])
            parts[k].wait_recv()
            passes.append(
                send(part.at[sl], beyond.at[sl], pass_ss.at[k], pass_rs.at[k], (source, n))
            )
        if k < EARLY:
            start, size = early_chunks[k]
            sl, row = pl.ds(start, size), rows_of(size)
            coeff = c_ref[sl]
            square, twice = coeff * coeff, 2.0 * coeff
            own_near, own_far = xv[sl, near], xv[sl, far]
            plane = in_plane(
                own_near, edge_r[0, sl][:, None, :], edge_r[1, sl][:, None, :], row, coeff
            )
            raws[k].wait_recv()
            raw_near, raw_far = raw[sl, far], raw[sl, near]
            sums_s[sl, far] = twice * plane + square * (own_far + raw_near)
            plane = in_plane(
                raw_near, corner_r[0, sl][:, None, :], corner_r[1, sl][:, None, :], row, coeff
            )
            sums_s[sl, near] = twice * plane + square * (own_near + raw_far)
            sums.append(
                send(sums_s.at[sl], sums_r.at[sl], sums_ss.at[k], sums_rs.at[k], (partner, n))
            )

    for copy in rests:
        copy.wait_recv()
    for start, size in pieces(nspec, EARLY + LATE):
        sl, row = pl.ds(start, size), rows_of(size)
        coeff = c_ref[sl]
        square, twice = coeff * coeff, 2.0 * coeff

        def halo(low, high, low_inner, high_inner):
            low, high, low_inner, high_inner = (
                v[:, None, :] for v in (low, high, low_inner, high_inner)
            )
            tile = jnp.where(row == 0, high, high_inner)
            return jnp.where(row == cy - 1, low, jnp.where(row == cy - 2, low_inner, tile))

        own = xv[sl, near], xv[sl, far]
        halos = (
            halo(edge_r[0, sl], edge_r[1, sl], rest_r[0, 1, sl], rest_r[1, 1, sl]),
            halo(rest_r[0, 0, sl], rest_r[1, 0, sl], rest_r[0, 2, sl], rest_r[1, 2, sl]),
        )
        for i, at in enumerate((near, far)):
            mine, side = own[i], halos[i]
            centre = in_plane(mine, *rolled(side), row, coeff) + twice * own[1 - i]
            edge = in_plane(side, *rolled(mine), row, coeff) + twice * halos[1 - i]
            out_ref[sl, at] = in_plane(centre, *rolled(edge), row, coeff) + 2.0 * square * mine

    for copy in touches:
        copy.wait_recv()
    for k in range(max(EARLY, LATE)):
        if k < EARLY:
            sl = pl.ds(*early_chunks[k])
            sums[k].wait_recv()
            out_ref[sl] = out_ref[sl] + sums_r[sl]
        if k < LATE:
            start, size = late_chunks[k]
            sl, to, row = pl.ds(start, size), pl.ds(early + start, size), rows_of(size)
            coeff = c_ref[to]
            square, twice = coeff * coeff, 2.0 * coeff
            close, second = part[sl, far], part[sl, near]
            plane = twice * in_plane(
                close, touch_r[0, 0, sl][:, None, :], touch_r[1, 0, sl][:, None, :], row, coeff
            )
            passes[k].wait_recv()
            ahead, third = beyond[sl, near], beyond[sl, far]
            out_ref[to, near] = out_ref[to, near] + plane + square * (second + ahead)
            plane = twice * in_plane(
                ahead, touch_r[0, 1, sl][:, None, :], touch_r[1, 1, sl][:, None, :], row, coeff
            )
            out_ref[to, far] = out_ref[to, far] + plane + square * (third + close)
    for copy in corners + edges + rests + touches + raws + parts + sums + passes:
        copy.wait_send()


def two_parts(values):
    high = values.astype(jnp.bfloat16)
    return high, (values - high.astype(jnp.float32)).astype(jnp.bfloat16)


def reaction(
    marks_ref, mixed_ref, heat_ref, logs_ref, sums_ref, out_ref,
    picked, temps, stacked, slots,
):
    nspec = mixed_ref.shape[0] // heat_ref.shape[0]
    stacks, height = heat_ref.shape
    per_row = marks_ref.shape[1]
    room = stacked.shape[0] // 4
    pad = sums_ref.shape[0] // 2
    out_ref[...] = mixed_ref[...]
    for k in range(BURN_MAX):
        slots[k] = 0
    count = jnp.int32(0)
    for i in range(stacks):
        burning = marks_ref[i // per_row, i % per_row]

        @pl.when((burning == 1) & (count < BURN_MAX))
        def _():
            slots[count] = i

        count = count + burning
    for k in range(BURN_MAX):
        cells = pl.ds(k * height, height)
        picked[:, cells] = mixed_ref[pl.ds(slots[k], nspec, stride=stacks), :]
        temps[:, cells] = heat_ref[pl.ds(slots[k], 1), :]
    stacked[...] = jnp.zeros_like(stacked)
    t, one = three_parts(1.0 / temps[...]), jnp.ones(temps.shape, jnp.float32)
    extra = (one, one, one, t[0], t[1], t[0], t[1], t[2], t[0])
    extra = rows_by_index((16, temps.shape[1]), extra)
    stacked[2 * room : 2 * room + 16, :] = extra.astype(jnp.bfloat16)
    values = picked[...]
    for substep in range(2):
        high, low = two_parts(jnp.log(values))
        stacked[0:nspec, :] = high
        stacked[room : room + nspec, :] = low
        expo = jnp.dot(logs_ref[...], stacked[...], preferred_element_type=jnp.float32)
        high, low = two_parts(jnp.exp(expo))
        total = jnp.dot(sums_ref[...], high, preferred_element_type=jnp.float32)
        total = total + jnp.dot(sums_ref[...], low, preferred_element_type=jnp.float32)
        gain, loss = total[0:nspec], total[pad : pad + nspec]
        values = values * (values + 0.5 * gain) / (values + 0.5 * loss)
    picked[...] = values
    for k in range(BURN_MAX):

        @pl.when(k < count)
        def _():
            column = picked[:, k * height : (k + 1) * height]
            out_ref[pl.ds(slots[k], nspec, stride=stacks), :] = column


def round_up(value, step):
    return -(-value // step) * step


def shards(
    n_wide,
    n_narrow,
    chemical_fractions,
    thermal_state,
    ignited_stacks,
    spreading_number,
    natural_exponent_scale,
    arrhenius_energy,
    incoming_stoichiometry,
    outgoing_stoichiometry,
):
    shape = chemical_fractions.shape
    nspec, cx, cy, height = shape
    nreact = incoming_stoichiometry.shape[0]
    f32, bf16 = jnp.float32, jnp.bfloat16
    vmem = pl.BlockSpec(memory_space=pltpu.VMEM)
    smem = pl.BlockSpec(memory_space=pltpu.SMEM)
    hbm = pl.BlockSpec(memory_space=pltpu.HBM)
    room, rows = round_up(nspec, 64), round_up(nreact, 16)
    pad, wide = round_up(nspec, 8), round_up(nreact, 128)
    dma = pltpu.SemaphoreType.DMA
    early = nspec // 16 * 8
    mixed, marks, logs_mat, sums_mat = pl.pallas_call(
        functools.partial(exchange, n_wide, n_narrow),
        out_shape=[
            jax.ShapeDtypeStruct(shape, f32),
            jax.ShapeDtypeStruct(ignited_stacks.shape, jnp.int32),
            jax.ShapeDtypeStruct((rows, 4 * room), bf16),
            jax.ShapeDtypeStruct((2 * pad, rows), bf16),
        ],
        in_specs=[hbm] * 7,
        out_specs=[vmem] * 4,
        scratch_shapes=[
            pltpu.SMEM((1, nspec), f32),
            *[pltpu.VMEM((nreact,), f32)] * 2,
            *[pltpu.VMEM((nspec, nreact), jnp.int32)] * 2,
            pltpu.VMEM((4 * room, wide), f32),
            pltpu.VMEM((nspec, 1, height), f32),
            dma((6,)),
            pltpu.VMEM(shape, f32),
            *[pltpu.VMEM((early,) + shape[1:], f32)] * 3,
            *[pltpu.VMEM((nspec - early,) + shape[1:], f32)] * 2,
            *[pltpu.VMEM((2, early, height), f32)] * 2,
            *[pltpu.VMEM((2, 2, nspec - early, height), f32)] * 2,
            *[pltpu.VMEM((2, nspec, height), f32)] * 2,
            *[pltpu.VMEM((2, 3, nspec, height), f32)] * 2,
            dma(()),
            *[dma((EARLY,))] * 4,
            *[dma((LATE,))] * 4,
            *[dma((10,))] * 2,
        ],
        compiler_params=pltpu.CompilerParams(
            collective_id=0, has_side_effects=True, vmem_limit_bytes=53 * 2**20
        ),
        name="exchange",
    )(
        chemical_fractions,
        spreading_number[None],
        ignited_stacks,
        natural_exponent_scale,
        arrhenius_energy,
        incoming_stoichiometry.T,
        outgoing_stoichiometry.T,
    )

    cells = BURN_MAX * height
    updated = pl.pallas_call(
        reaction,
        out_shape=jax.ShapeDtypeStruct((nspec * cx * cy, height), f32),
        in_specs=[smem] + [vmem] * 4,
        out_specs=vmem,
        scratch_shapes=[
            pltpu.VMEM((nspec, cells), f32),
            pltpu.VMEM((1, cells), f32),
            pltpu.VMEM((4 * room, cells), bf16),
            pltpu.SMEM((BURN_MAX,), jnp.int32),
        ],
        compiler_params=pltpu.CompilerParams(vmem_limit_bytes=32 * 2**20),
        name="reaction",
    )(
        marks,
        mixed.reshape(nspec * cx * cy, height),
        thermal_state.reshape(cx * cy, height),
        logs_mat,
        sums_mat,
    )
    return updated.reshape(shape)


def solution(mesh):
    in_specs = (
        P(None, "wide", "narrow", None),
        P("wide", "narrow", None),
        P("wide", "narrow"),
        P(),
        P(),
        P(),
        P(),
        P(),
    )
    out_specs = P(None, "wide", "narrow", None)
    body = functools.partial(shards, mesh.shape["wide"], mesh.shape["narrow"])
    return jax.shard_map(body, mesh=mesh, in_specs=in_specs, out_specs=out_specs, check_vma=False)
```

```python
import functools

import jax
import jax.numpy as jnp
from jax import lax
from jax.experimental import pallas as pl
from jax.experimental.pallas import tpu as pltpu
from jax.sharding import PartitionSpec as P

BURN_MAX = 8
EARLY = 3
LATE = 3
MESH = pl.DeviceIdType.MESH


def pieces(total, count):
    edges = [total * i // count for i in range(count + 1)]
    return [(lo, hi - lo) for lo, hi in zip(edges[:-1], edges[1:])]


def in_plane(centre, up_edge, down_edge, row, coeff):
    last = centre.shape[1] - 1
    beside = jnp.where(row == 0, up_edge, pltpu.roll(centre, 1, 1))
    beside = beside + jnp.where(row == last, down_edge, pltpu.roll(centre, last, 1))
    beside = beside + pltpu.roll(centre, 1, 2) + pltpu.roll(centre, centre.shape[2] - 1, 2)
    return centre + coeff * (beside - 6.0 * centre)


def rolled(tile):
    return pltpu.roll(tile, 1, 1), pltpu.roll(tile, tile.shape[1] - 1, 1)


def three_parts(values):
    parts = []
    for _ in range(3):
        parts.append(values.astype(jnp.bfloat16).astype(jnp.float32))
        values = values - parts[-1]
    return parts


def rows_by_index(shape, rows):
    index = lax.broadcasted_iota(jnp.int32, shape, 0)
    block = jnp.zeros(shape, jnp.float32)
    for i, row in enumerate(rows):
        block = jnp.where(index == i, row, block)
    return block


def prepare(scale_ref, energy_ref, incoming_ref, outgoing_ref, work, logs_ref, sums_ref):
    nspec, nreact = incoming_ref.shape
    room, pad = logs_ref.shape[1] // 4, sums_ref.shape[0] // 2
    rows = logs_ref.shape[0]
    incoming = incoming_ref[...].astype(jnp.float32)
    work[...] = jnp.zeros_like(work)
    work[0:nspec, 0:nreact] = outgoing_ref[...].astype(jnp.float32)
    work[pad : pad + nspec, 0:nreact] = incoming
    sums_ref[...] = work[0 : 2 * pad, 0:rows].astype(jnp.bfloat16)
    work[...] = jnp.zeros_like(work)
    work[0:nspec, 0:nreact] = incoming
    work[room : room + nspec, 0:nreact] = incoming
    a, e = three_parts(scale_ref[...][None]), three_parts(-energy_ref[...][None])
    extra = (a[0], a[1], a[2], e[0], e[0], e[1], e[1], e[0], e[2])
    work[2 * room : 2 * room + 16, 0:nreact] = rows_by_index((16, nreact), extra)
    logs_ref[...] = work[...].T[0:rows].astype(jnp.bfloat16)


def exchange(
    n_wide, n_narrow, x_ref, coeff_hbm, scale_hbm, energy_hbm, incoming_hbm,
    outgoing_hbm, out_hbm, logs_hbm, sums_hbm, out_ref, logs_ref, sums_ref, store_sem, coeff_ref, scale_ref, energy_ref,
    incoming_ref, outgoing_ref, work, c_ref, load_sem, xv, raw, sums_s, sums_r, part, beyond,
    corner_s, corner_r, touch_s, touch_r, edge_s, edge_r, rest_s, rest_r, local_sem,
    raw_ss, raw_rs, sums_ss, sums_rs, part_ss, part_rs, pass_ss, pass_rs, side_ss, side_rs,
):
    w, n = lax.axis_index("wide"), lax.axis_index("narrow")
    odd = w % 2
    near, far = 1 - odd, odd
    partner = w + 1 - 2 * odd
    other = (w + n_wide + 2 * odd - 1) % n_wide
    target = (w + n_wide + 4 * odd - 2) % n_wide
    source = (w + n_wide + 2 - 4 * odd) % n_wide
    left, right = (n + n_narrow - 1) % n_narrow, (n + 1) % n_narrow
    nspec, _, cy, _ = xv.shape
    early, late = raw.shape[0], part.shape[0]
    early_chunks, late_chunks = pieces(early, EARLY), pieces(late, LATE)

    load = pltpu.make_async_copy(x_ref, xv, local_sem)
    load.start()
    loads = [
        pltpu.make_async_copy(src, dst, load_sem.at[i])
        for i, (src, dst) in enumerate((
            (coeff_hbm, coeff_ref), (scale_hbm, scale_ref), (energy_hbm, energy_ref),
            (incoming_hbm, incoming_ref), (outgoing_hbm, outgoing_ref),
        ))
    ]
    for copy in loads:
        copy.start()
    barrier = pltpu.get_barrier_semaphore()
    greeted = [(w, left), (w, right)]
    greeted += [(a, b) for a in (source, partner) for b in (n, left, right)]
    greeted += [(other, left), (other, right), (target, n)]
    for device in greeted:
        pl.semaphore_signal(barrier, inc=1, device_id=device, device_id_type=MESH)
    load.wait()
    for side, (row, inner) in enumerate(((cy - 1, cy - 2), (0, 1))):
        corner_s[side] = xv[0:early, far, row, :]
        touch_s[side, 0] = xv[early:nspec, near, row, :]
        touch_s[side, 1] = xv[early:nspec, far, row, :]
        edge_s[side] = xv[:, near, row, :]
        rest_s[side, 0] = xv[:, far, row, :]
        rest_s[side, 1] = xv[:, near, inner, :]
        rest_s[side, 2] = xv[:, far, inner, :]
    pl.semaphore_wait(barrier, len(greeted))

    def send(src, dst, ss, rs, device):
        copy = pltpu.make_async_remote_copy(
            src_ref=src, dst_ref=dst, send_sem=ss, recv_sem=rs,
            device_id=device, device_id_type=MESH,
        )
        copy.start()
        return copy

    def sides_of(at, src, dst, row):
        return [
            send(src(side), dst(side), side_ss.at[at + side], side_rs.at[at + side], (row, to))
            for side, to in enumerate((right, left))
        ]

    corners = sides_of(0, lambda i: corner_s.at[i], lambda i: corner_r.at[i], target)
    edges = sides_of(2, lambda i: edge_s.at[i], lambda i: edge_r.at[i], w)
    raws, parts = [], []
    for k in range(max(EARLY, LATE)):
        if k < EARLY:
            sl = pl.ds(*early_chunks[k])
            raws.append(send(xv.at[sl], raw.at[sl], raw_ss.at[k], raw_rs.at[k], (target, n)))
        if k < LATE:
            start, size = late_chunks[k]
            parts.append(
                send(
                    xv.at[pl.ds(early + start, size)], part.at[pl.ds(start, size)],
                    part_ss.at[k], part_rs.at[k], (partner, n),
                )
            )
    rests = sides_of(4, lambda i: rest_s.at[i], lambda i: rest_r.at[i], w)
    touches = sides_of(6, lambda i: touch_s.at[i, 0], lambda i: touch_r.at[i, 0], partner)
    touches += sides_of(8, lambda i: touch_s.at[i, 1], lambda i: touch_r.at[i, 1], other)
    for copy in loads:
        copy.wait()
    for i in range(nspec):
        c_ref[i] = jnp.full(c_ref.shape[1:], coeff_ref[0, i], jnp.float32)
    prepare(scale_ref, energy_ref, incoming_ref, outgoing_ref, work, logs_ref, sums_ref)
    stores = []

    def store(src, dst):
        stores.append(pltpu.make_async_copy(src, dst, store_sem.at[len(stores)]))
        stores[-1].start()

    store(logs_ref, logs_hbm)
    store(sums_ref, sums_hbm)
    for copy in corners + edges:
        copy.wait_recv()

    def rows_of(size):
        return lax.broadcasted_iota(jnp.int32, (size,) + xv.shape[2:], 1)

    sums, passes = [], []
    for k in range(max(EARLY, LATE)):
        if k < LATE:
            sl = pl.ds(*late_chunks[k])
            parts[k].wait_recv()
            passes.append(
                send(part.at[sl], beyond.at[sl], pass_ss.at[k], pass_rs.at[k], (source, n))
            )
        if k < EARLY:
            start, size = early_chunks[k]
            sl, row = pl.ds(start, size), rows_of(size)
            coeff = c_ref[sl]
            square, twice = coeff * coeff, 2.0 * coeff
            own_near, own_far = xv[sl, near], xv[sl, far]
            plane = in_plane(
                own_near, edge_r[0, sl][:, None, :], edge_r[1, sl][:, None, :], row, coeff
            )
            raws[k].wait_recv()
            raw_near, raw_far = raw[sl, far], raw[sl, near]
            sums_s[sl, far] = twice * plane + square * (own_far + raw_near)
            plane = in_plane(
                raw_near, corner_r[0, sl][:, None, :], corner_r[1, sl][:, None, :], row, coeff
            )
            sums_s[sl, near] = twice * plane + square * (own_near + raw_far)
            sums.append(
                send(sums_s.at[sl], sums_r.at[sl], sums_ss.at[k], sums_rs.at[k], (partner, n))
            )

    for copy in rests:
        copy.wait_recv()
    for start, size in pieces(nspec, EARLY + LATE):
        sl, row = pl.ds(start, size), rows_of(size)
        coeff = c_ref[sl]
        square, twice = coeff * coeff, 2.0 * coeff

        def halo(low, high, low_inner, high_inner):
            low, high, low_inner, high_inner = (
                v[:, None, :] for v in (low, high, low_inner, high_inner)
            )
            tile = jnp.where(row == 0, high, high_inner)
            return jnp.where(row == cy - 1, low, jnp.where(row == cy - 2, low_inner, tile))

        own = xv[sl, near], xv[sl, far]
        halos = (
            halo(edge_r[0, sl], edge_r[1, sl], rest_r[0, 1, sl], rest_r[1, 1, sl]),
            halo(rest_r[0, 0, sl], rest_r[1, 0, sl], rest_r[0, 2, sl], rest_r[1, 2, sl]),
        )
        for i, at in enumerate((near, far)):
            mine, side = own[i], halos[i]
            centre = in_plane(mine, *rolled(side), row, coeff) + twice * own[1 - i]
            edge = in_plane(side, *rolled(mine), row, coeff) + twice * halos[1 - i]
            out_ref[sl, at] = in_plane(centre, *rolled(edge), row, coeff) + 2.0 * square * mine

    for copy in touches:
        copy.wait_recv()
    for k in range(max(EARLY, LATE)):
        if k < EARLY:
            sl = pl.ds(*early_chunks[k])
            sums[k].wait_recv()
            out_ref[sl] = out_ref[sl] + sums_r[sl]
            store(out_ref.at[sl], out_hbm.at[sl])
        if k < LATE:
            start, size = late_chunks[k]
            sl, to, row = pl.ds(start, size), pl.ds(early + start, size), rows_of(size)
            coeff = c_ref[to]
            square, twice = coeff * coeff, 2.0 * coeff
            close, second = part[sl, far], part[sl, near]
            plane = twice * in_plane(
                close, touch_r[0, 0, sl][:, None, :], touch_r[1, 0, sl][:, None, :], row, coeff
            )
            passes[k].wait_recv()
            ahead, third = beyond[sl, near], beyond[sl, far]
            out_ref[to, near] = out_ref[to, near] + plane + square * (second + ahead)
            plane = twice * in_plane(
                ahead, touch_r[0, 1, sl][:, None, :], touch_r[1, 1, sl][:, None, :], row, coeff
            )
            out_ref[to, far] = out_ref[to, far] + plane + square * (third + close)
            store(out_ref.at[to], out_hbm.at[to])
    for copy in corners + edges + rests + touches + raws + parts + sums + passes:
        copy.wait_send()
    for copy in stores:
        copy.wait()


def two_parts(values):
    high = values.astype(jnp.bfloat16)
    return high, (values - high.astype(jnp.float32)).astype(jnp.bfloat16)


def reaction(
    marks_hbm, mixed_hbm, heat_hbm, logs_hbm, sums_hbm, out_ref,
    marks_ref, heat_ref, logs_ref, sums_ref, sems, picked, temps, stacked, slots,
):
    loads = [
        pltpu.make_async_copy(src, dst, sems.at[i])
        for i, (src, dst) in enumerate((
            (marks_hbm, marks_ref), (heat_hbm, heat_ref), (mixed_hbm, out_ref),
            (logs_hbm, logs_ref), (sums_hbm, sums_ref),
        ))
    ]
    for copy in loads:
        copy.start()
    nspec = out_ref.shape[0] // heat_ref.shape[0]
    stacks, height = heat_ref.shape
    per_row = marks_ref.shape[1]
    room = stacked.shape[0] // 4
    pad = sums_ref.shape[0] // 2
    stacked[...] = jnp.zeros_like(stacked)
    for k in range(BURN_MAX):
        slots[k] = 0
    loads[0].wait()
    count = jnp.int32(0)
    for i in range(stacks):
        burning = marks_ref[i // per_row, i % per_row]

        @pl.when((burning == 1) & (count < BURN_MAX))
        def _():
            slots[count] = i

        count = count + burning
    for copy in loads[1:]:
        copy.wait()
    for k in range(BURN_MAX):
        cells = pl.ds(k * height, height)
        picked[:, cells] = out_ref[pl.ds(slots[k], nspec, stride=stacks), :]
        temps[:, cells] = heat_ref[pl.ds(slots[k], 1), :]
    t, one = three_parts(1.0 / temps[...]), jnp.ones(temps.shape, jnp.float32)
    extra = (one, one, one, t[0], t[1], t[0], t[1], t[2], t[0])
    extra = rows_by_index((16, temps.shape[1]), extra)
    stacked[2 * room : 2 * room + 16, :] = extra.astype(jnp.bfloat16)
    values = picked[...]
    for substep in range(2):
        high, low = two_parts(jnp.log(values))
        stacked[0:nspec, :] = high
        stacked[room : room + nspec, :] = low
        expo = jnp.dot(logs_ref[...], stacked[...], preferred_element_type=jnp.float32)
        high, low = two_parts(jnp.exp(expo))
        total = jnp.dot(sums_ref[...], high, preferred_element_type=jnp.float32)
        total = total + jnp.dot(sums_ref[...], low, preferred_element_type=jnp.float32)
        gain, loss = total[0:nspec], total[pad : pad + nspec]
        values = values * (values + 0.5 * gain) / (values + 0.5 * loss)
    picked[...] = values
    for k in range(BURN_MAX):

        @pl.when(k < count)
        def _():
            column = picked[:, k * height : (k + 1) * height]
            out_ref[pl.ds(slots[k], nspec, stride=stacks), :] = column


def round_up(value, step):
    return -(-value // step) * step


def shards(
    n_wide,
    n_narrow,
    chemical_fractions,
    thermal_state,
    ignited_stacks,
    spreading_number,
    natural_exponent_scale,
    arrhenius_energy,
    incoming_stoichiometry,
    outgoing_stoichiometry,
):
    shape = chemical_fractions.shape
    nspec, cx, cy, height = shape
    nreact = incoming_stoichiometry.shape[0]
    f32, bf16 = jnp.float32, jnp.bfloat16
    vmem = pl.BlockSpec(memory_space=pltpu.VMEM)
    hbm = pl.BlockSpec(memory_space=pltpu.HBM)
    room, rows = round_up(nspec, 64), round_up(nreact, 16)
    pad, wide = round_up(nspec, 8), round_up(nreact, 128)
    dma = pltpu.SemaphoreType.DMA
    early = nspec // 16 * 8
    mixed, logs_mat, sums_mat = pl.pallas_call(
        functools.partial(exchange, n_wide, n_narrow),
        out_shape=[
            jax.ShapeDtypeStruct(shape, f32),
            jax.ShapeDtypeStruct((rows, 4 * room), bf16),
            jax.ShapeDtypeStruct((2 * pad, rows), bf16),
        ],
        in_specs=[hbm] * 6,
        out_specs=[hbm] * 3,
        scratch_shapes=[
            pltpu.VMEM(shape, f32),
            pltpu.VMEM((rows, 4 * room), bf16),
            pltpu.VMEM((2 * pad, rows), bf16),
            dma((EARLY + LATE + 2,)),
            pltpu.SMEM((1, nspec), f32),
            *[pltpu.VMEM((nreact,), f32)] * 2,
            *[pltpu.VMEM((nspec, nreact), jnp.int32)] * 2,
            pltpu.VMEM((4 * room, wide), f32),
            pltpu.VMEM((nspec, 1, height), f32),
            dma((5,)),
            pltpu.VMEM(shape, f32),
            *[pltpu.VMEM((early,) + shape[1:], f32)] * 3,
            *[pltpu.VMEM((nspec - early,) + shape[1:], f32)] * 2,
            *[pltpu.VMEM((2, early, height), f32)] * 2,
            *[pltpu.VMEM((2, 2, nspec - early, height), f32)] * 2,
            *[pltpu.VMEM((2, nspec, height), f32)] * 2,
            *[pltpu.VMEM((2, 3, nspec, height), f32)] * 2,
            dma(()),
            *[dma((EARLY,))] * 4,
            *[dma((LATE,))] * 4,
            *[dma((10,))] * 2,
        ],
        compiler_params=pltpu.CompilerParams(
            collective_id=0, has_side_effects=True, vmem_limit_bytes=60 * 2**20
        ),
        name="exchange",
    )(
        chemical_fractions,
        spreading_number[None],
        natural_exponent_scale,
        arrhenius_energy,
        incoming_stoichiometry.T,
        outgoing_stoichiometry.T,
    )

    cells = BURN_MAX * height
    updated = pl.pallas_call(
        reaction,
        out_shape=jax.ShapeDtypeStruct((nspec * cx * cy, height), f32),
        in_specs=[hbm] * 5,
        out_specs=vmem,
        scratch_shapes=[
            pltpu.SMEM(ignited_stacks.shape, jnp.int32),
            pltpu.VMEM((cx * cy, height), f32),
            pltpu.VMEM((rows, 4 * room), bf16),
            pltpu.VMEM((2 * pad, rows), bf16),
            dma((5,)),
            pltpu.VMEM((nspec, cells), f32),
            pltpu.VMEM((1, cells), f32),
            pltpu.VMEM((4 * room, cells), bf16),
            pltpu.SMEM((BURN_MAX,), jnp.int32),
        ],
        compiler_params=pltpu.CompilerParams(vmem_limit_bytes=60 * 2**20),
        name="reaction",
    )(
        ignited_stacks,
        mixed.reshape(nspec * cx * cy, height),
        thermal_state.reshape(cx * cy, height),
        logs_mat,
        sums_mat,
    )
    return updated.reshape(shape)


def solution(mesh):
    in_specs = (
        P(None, "wide", "narrow", None),
        P("wide", "narrow", None),
        P("wide", "narrow"),
        P(),
        P(),
        P(),
        P(),
        P(),
    )
    out_specs = P(None, "wide", "narrow", None)
    body = functools.partial(shards, mesh.shape["wide"], mesh.shape["narrow"])
    return jax.shard_map(body, mesh=mesh, in_specs=in_specs, out_specs=out_specs, check_vma=False)
```

```python
import functools

import jax
import jax.numpy as jnp
from jax import lax
from jax.experimental import pallas as pl
from jax.experimental.pallas import tpu as pltpu
from jax.sharding import PartitionSpec as P

BURN_MAX = 8
EARLY = 3
LATE = 3
MESH = pl.DeviceIdType.MESH


def pieces(total, count):
    edges = [total * i // count for i in range(count + 1)]
    return [(lo, hi - lo) for lo, hi in zip(edges[:-1], edges[1:])]


def in_plane(centre, up_edge, down_edge, row, coeff):
    last = centre.shape[1] - 1
    beside = jnp.where(row == 0, up_edge, pltpu.roll(centre, 1, 1))
    beside = beside + jnp.where(row == last, down_edge, pltpu.roll(centre, last, 1))
    beside = beside + pltpu.roll(centre, 1, 2) + pltpu.roll(centre, centre.shape[2] - 1, 2)
    return centre + coeff * (beside - 6.0 * centre)


def rolled(tile):
    return pltpu.roll(tile, 1, 1), pltpu.roll(tile, tile.shape[1] - 1, 1)


def three_parts(values):
    parts = []
    for _ in range(3):
        parts.append(values.astype(jnp.bfloat16).astype(jnp.float32))
        values = values - parts[-1]
    return parts


def rows_by_index(shape, rows):
    index = lax.broadcasted_iota(jnp.int32, shape, 0)
    block = jnp.zeros(shape, jnp.float32)
    for i, row in enumerate(rows):
        block = jnp.where(index == i, row, block)
    return block


def prepare(scale_ref, energy_ref, incoming_ref, outgoing_ref, work, logs_ref, sums_ref):
    nspec, nreact = incoming_ref.shape
    room, pad = logs_ref.shape[1] // 4, sums_ref.shape[0] // 2
    rows = logs_ref.shape[0]
    incoming = incoming_ref[...].astype(jnp.float32)
    work[...] = jnp.zeros_like(work)
    work[0:nspec, 0:nreact] = outgoing_ref[...].astype(jnp.float32)
    work[pad : pad + nspec, 0:nreact] = incoming
    sums_ref[...] = work[0 : 2 * pad, 0:rows].astype(jnp.bfloat16)
    work[...] = jnp.zeros_like(work)
    work[0:nspec, 0:nreact] = incoming
    work[room : room + nspec, 0:nreact] = incoming
    a, e = three_parts(scale_ref[...][None]), three_parts(-energy_ref[...][None])
    extra = (a[0], a[1], a[2], e[0], e[0], e[1], e[1], e[0], e[2])
    work[2 * room : 2 * room + 16, 0:nreact] = rows_by_index((16, nreact), extra)
    logs_ref[...] = work[...].T[0:rows].astype(jnp.bfloat16)


def exchange(
    n_wide, n_narrow, x_ref, coeff_hbm, scale_hbm, energy_hbm, incoming_hbm,
    outgoing_hbm, out_hbm, logs_hbm, sums_hbm, out_ref, logs_ref, sums_ref, store_sem, coeff_ref, scale_ref, energy_ref,
    incoming_ref, outgoing_ref, work, c_ref, load_sem, xv, raw, sums_s, sums_r, part, beyond,
    corner_s, corner_r, touch_s, touch_r, edge_s, edge_r, rest_s, rest_r, local_sem,
    raw_ss, raw_rs, sums_ss, sums_rs, part_ss, part_rs, pass_ss, pass_rs, side_ss, side_rs,
):
    w, n = lax.axis_index("wide"), lax.axis_index("narrow")
    odd = w % 2
    near, far = 1 - odd, odd
    partner = w + 1 - 2 * odd
    other = (w + n_wide + 2 * odd - 1) % n_wide
    target = (w + n_wide + 4 * odd - 2) % n_wide
    source = (w + n_wide + 2 - 4 * odd) % n_wide
    left, right = (n + n_narrow - 1) % n_narrow, (n + 1) % n_narrow
    nspec, _, cy, _ = xv.shape
    early, late = raw.shape[0], part.shape[0]
    early_chunks, late_chunks = pieces(early, EARLY), pieces(late, LATE)

    load = pltpu.make_async_copy(x_ref, xv, local_sem)
    load.start()
    loads = [
        pltpu.make_async_copy(src, dst, load_sem.at[i])
        for i, (src, dst) in enumerate((
            (coeff_hbm, coeff_ref), (scale_hbm, scale_ref), (energy_hbm, energy_ref),
            (incoming_hbm, incoming_ref), (outgoing_hbm, outgoing_ref),
        ))
    ]
    for copy in loads:
        copy.start()
    barrier = pltpu.get_barrier_semaphore()
    greeted = [(w, left), (w, right)]
    greeted += [(a, b) for a in (source, partner) for b in (n, left, right)]
    greeted += [(other, left), (other, right), (target, n)]
    for device in greeted:
        pl.semaphore_signal(barrier, inc=1, device_id=device, device_id_type=MESH)
    load.wait()
    for side, (row, inner) in enumerate(((cy - 1, cy - 2), (0, 1))):
        corner_s[side] = xv[0:early, far, row, :]
        touch_s[side, 0] = xv[early:nspec, near, row, :]
        touch_s[side, 1] = xv[early:nspec, far, row, :]
        edge_s[side] = xv[:, near, row, :]
        rest_s[side, 0] = xv[:, far, row, :]
        rest_s[side, 1] = xv[:, near, inner, :]
        rest_s[side, 2] = xv[:, far, inner, :]
    pl.semaphore_wait(barrier, len(greeted))

    def send(src, dst, ss, rs, device):
        copy = pltpu.make_async_remote_copy(
            src_ref=src, dst_ref=dst, send_sem=ss, recv_sem=rs,
            device_id=device, device_id_type=MESH,
        )
        copy.start()
        return copy

    def sides_of(at, src, dst, row):
        return [
            send(src(side), dst(side), side_ss.at[at + side], side_rs.at[at + side], (row, to))
            for side, to in enumerate((right, left))
        ]

    corners = sides_of(0, lambda i: corner_s.at[i], lambda i: corner_r.at[i], target)
    edges = sides_of(2, lambda i: edge_s.at[i], lambda i: edge_r.at[i], w)
    raws, parts = [], []
    for k in range(max(EARLY, LATE)):
        if k < EARLY:
            sl = pl.ds(*early_chunks[k])
            raws.append(send(xv.at[sl], raw.at[sl], raw_ss.at[k], raw_rs.at[k], (target, n)))
        if k < LATE:
            start, size = late_chunks[k]
            parts.append(
                send(
                    xv.at[pl.ds(early + start, size)], part.at[pl.ds(start, size)],
                    part_ss.at[k], part_rs.at[k], (partner, n),
                )
            )
    rests = sides_of(4, lambda i: rest_s.at[i], lambda i: rest_r.at[i], w)
    touches = sides_of(6, lambda i: touch_s.at[i, 0], lambda i: touch_r.at[i, 0], partner)
    touches += sides_of(8, lambda i: touch_s.at[i, 1], lambda i: touch_r.at[i, 1], other)
    for copy in loads:
        copy.wait()
    for i in range(nspec):
        c_ref[i] = jnp.full(c_ref.shape[1:], coeff_ref[0, i], jnp.float32)
    prepare(scale_ref, energy_ref, incoming_ref, outgoing_ref, work, logs_ref, sums_ref)
    stores = []

    def store(src, dst):
        stores.append(pltpu.make_async_copy(src, dst, store_sem.at[len(stores)]))
        stores[-1].start()

    store(logs_ref, logs_hbm)
    store(sums_ref, sums_hbm)
    for copy in corners + edges:
        copy.wait_recv()

    def rows_of(size):
        return lax.broadcasted_iota(jnp.int32, (size,) + xv.shape[2:], 1)

    sums, passes = [], []
    for k in range(max(EARLY, LATE)):
        if k < LATE:
            sl = pl.ds(*late_chunks[k])
            parts[k].wait_recv()
            passes.append(
                send(part.at[sl], beyond.at[sl], pass_ss.at[k], pass_rs.at[k], (source, n))
            )
        if k < EARLY:
            start, size = early_chunks[k]
            sl, row = pl.ds(start, size), rows_of(size)
            coeff = c_ref[sl]
            square, twice = coeff * coeff, 2.0 * coeff
            own_near, own_far = xv[sl, near], xv[sl, far]
            plane = in_plane(
                own_near, edge_r[0, sl][:, None, :], edge_r[1, sl][:, None, :], row, coeff
            )
            raws[k].wait_recv()
            raw_near, raw_far = raw[sl, far], raw[sl, near]
            sums_s[sl, far] = twice * plane + square * (own_far + raw_near)
            plane = in_plane(
                raw_near, corner_r[0, sl][:, None, :], corner_r[1, sl][:, None, :], row, coeff
            )
            sums_s[sl, near] = twice * plane + square * (own_near + raw_far)
            sums.append(
                send(sums_s.at[sl], sums_r.at[sl], sums_ss.at[k], sums_rs.at[k], (partner, n))
            )

    for copy in rests:
        copy.wait_recv()
    for start, size in pieces(nspec, EARLY + LATE):
        sl, row = pl.ds(start, size), rows_of(size)
        coeff = c_ref[sl]
        square, twice = coeff * coeff, 2.0 * coeff

        def halo(low, high, low_inner, high_inner):
            low, high, low_inner, high_inner = (
                v[:, None, :] for v in (low, high, low_inner, high_inner)
            )
            tile = jnp.where(row == 0, high, high_inner)
            return jnp.where(row == cy - 1, low, jnp.where(row == cy - 2, low_inner, tile))

        own = xv[sl, near], xv[sl, far]
        halos = (
            halo(edge_r[0, sl], edge_r[1, sl], rest_r[0, 1, sl], rest_r[1, 1, sl]),
            halo(rest_r[0, 0, sl], rest_r[1, 0, sl], rest_r[0, 2, sl], rest_r[1, 2, sl]),
        )
        for i, at in enumerate((near, far)):
            mine, side = own[i], halos[i]
            centre = in_plane(mine, *rolled(side), row, coeff) + twice * own[1 - i]
            edge = in_plane(side, *rolled(mine), row, coeff) + twice * halos[1 - i]
            out_ref[sl, at] = in_plane(centre, *rolled(edge), row, coeff) + 2.0 * square * mine

    for copy in touches:
        copy.wait_recv()
    for k in range(max(EARLY, LATE)):
        if k < EARLY:
            sl = pl.ds(*early_chunks[k])
            sums[k].wait_recv()
            out_ref[sl] = out_ref[sl] + sums_r[sl]
            store(out_ref.at[sl], out_hbm.at[sl])
        if k < LATE:
            start, size = late_chunks[k]
            sl, to, row = pl.ds(start, size), pl.ds(early + start, size), rows_of(size)
            coeff = c_ref[to]
            square, twice = coeff * coeff, 2.0 * coeff
            close, second = part[sl, far], part[sl, near]
            plane = twice * in_plane(
                close, touch_r[0, 0, sl][:, None, :], touch_r[1, 0, sl][:, None, :], row, coeff
            )
            passes[k].wait_recv()
            ahead, third = beyond[sl, near], beyond[sl, far]
            out_ref[to, near] = out_ref[to, near] + plane + square * (second + ahead)
            plane = twice * in_plane(
                ahead, touch_r[0, 1, sl][:, None, :], touch_r[1, 1, sl][:, None, :], row, coeff
            )
            out_ref[to, far] = out_ref[to, far] + plane + square * (third + close)
            store(out_ref.at[to], out_hbm.at[to])
    for copy in corners + edges + rests + touches + raws + parts + sums + passes:
        copy.wait_send()
    for copy in stores:
        copy.wait()


def two_parts(values):
    high = values.astype(jnp.bfloat16)
    return high, (values - high.astype(jnp.float32)).astype(jnp.bfloat16)


def reaction(
    marks_hbm, mixed_hbm, heat_hbm, logs_hbm, sums_hbm, out_ref,
    marks_ref, heat_ref, logs_ref, sums_ref, sems, picked, temps, stacked, slots,
):
    loads = [
        pltpu.make_async_copy(src, dst, sems.at[i])
        for i, (src, dst) in enumerate((
            (marks_hbm, marks_ref), (heat_hbm, heat_ref), (mixed_hbm, out_ref),
            (logs_hbm, logs_ref), (sums_hbm, sums_ref),
        ))
    ]
    for copy in loads:
        copy.start()
    nspec = out_ref.shape[0] // heat_ref.shape[0]
    stacks, height = heat_ref.shape
    per_row = marks_ref.shape[1]
    room = stacked.shape[0] // 4
    pad = sums_ref.shape[0] // 2
    stacked[...] = jnp.zeros_like(stacked)
    for k in range(BURN_MAX):
        slots[k] = 0
    loads[0].wait()
    count = jnp.int32(0)
    for i in range(stacks):
        burning = marks_ref[i // per_row, i % per_row]

        @pl.when((burning == 1) & (count < BURN_MAX))
        def _():
            slots[count] = i

        count = count + burning
    loads[1].wait()
    for k in range(BURN_MAX):
        temps[:, k * height : (k + 1) * height] = heat_ref[pl.ds(slots[k], 1), :]
    t, one = three_parts(1.0 / temps[...]), jnp.ones(temps.shape, jnp.float32)
    extra = (one, one, one, t[0], t[1], t[0], t[1], t[2], t[0])
    extra = rows_by_index((16, temps.shape[1]), extra)
    stacked[2 * room : 2 * room + 16, :] = extra.astype(jnp.bfloat16)
    whole = nspec // 8 * 8
    groups = [(0, whole)] + [(i, 1) for i in range(whole, nspec)]
    for copy in loads[2:]:
        copy.wait()
    for k in range(BURN_MAX):
        for first, size in groups:
            stride = stacks if size > 1 else None
            rows = pl.ds(slots[k] + first * stacks, size, stride=stride)
            picked[first : first + size, k * height : (k + 1) * height] = out_ref[rows, :]
    width = picked.shape[1] // 2
    halves = [slice(i * width, (i + 1) * width) for i in range(2)]
    values = [picked[:, cells] for cells in halves]
    for substep in range(2):
        for i, cells in enumerate(halves):
            high, low = two_parts(jnp.log(values[i]))
            stacked[0:nspec, cells] = high
            stacked[room : room + nspec, cells] = low
            expo = jnp.dot(logs_ref[...], stacked[:, cells], preferred_element_type=jnp.float32)
            high, low = two_parts(jnp.exp(expo))
            total = jnp.dot(sums_ref[...], high, preferred_element_type=jnp.float32)
            total = total + jnp.dot(sums_ref[...], low, preferred_element_type=jnp.float32)
            gain, loss = total[0:nspec], total[pad : pad + nspec]
            values[i] = values[i] * (values[i] + 0.5 * gain) / (values[i] + 0.5 * loss)
    for i, cells in enumerate(halves):
        picked[:, cells] = values[i]
    for k in range(BURN_MAX):

        @pl.when(k < count)
        def _():
            for first, size in groups:
                stride = stacks if size > 1 else None
                rows = pl.ds(slots[k] + first * stacks, size, stride=stride)
                column = picked[first : first + size, k * height : (k + 1) * height]
                out_ref[rows, :] = column


def round_up(value, step):
    return -(-value // step) * step


def shards(
    n_wide,
    n_narrow,
    chemical_fractions,
    thermal_state,
    ignited_stacks,
    spreading_number,
    natural_exponent_scale,
    arrhenius_energy,
    incoming_stoichiometry,
    outgoing_stoichiometry,
):
    shape = chemical_fractions.shape
    nspec, cx, cy, height = shape
    nreact = incoming_stoichiometry.shape[0]
    f32, bf16 = jnp.float32, jnp.bfloat16
    vmem = pl.BlockSpec(memory_space=pltpu.VMEM)
    hbm = pl.BlockSpec(memory_space=pltpu.HBM)
    room, rows = round_up(nspec, 64), round_up(nreact, 16)
    pad, wide = round_up(nspec, 8), round_up(nreact, 128)
    dma = pltpu.SemaphoreType.DMA
    early = nspec // 16 * 8
    mixed, logs_mat, sums_mat = pl.pallas_call(
        functools.partial(exchange, n_wide, n_narrow),
        out_shape=[
            jax.ShapeDtypeStruct(shape, f32),
            jax.ShapeDtypeStruct((rows, 4 * room), bf16),
            jax.ShapeDtypeStruct((2 * pad, rows), bf16),
        ],
        in_specs=[hbm] * 6,
        out_specs=[hbm] * 3,
        scratch_shapes=[
            pltpu.VMEM(shape, f32),
            pltpu.VMEM((rows, 4 * room), bf16),
            pltpu.VMEM((2 * pad, rows), bf16),
            dma((EARLY + LATE + 2,)),
            pltpu.SMEM((1, nspec), f32),
            *[pltpu.VMEM((nreact,), f32)] * 2,
            *[pltpu.VMEM((nspec, nreact), jnp.int32)] * 2,
            pltpu.VMEM((4 * room, wide), f32),
            pltpu.VMEM((nspec, 1, height), f32),
            dma((5,)),
            pltpu.VMEM(shape, f32),
            *[pltpu.VMEM((early,) + shape[1:], f32)] * 3,
            *[pltpu.VMEM((nspec - early,) + shape[1:], f32)] * 2,
            *[pltpu.VMEM((2, early, height), f32)] * 2,
            *[pltpu.VMEM((2, 2, nspec - early, height), f32)] * 2,
            *[pltpu.VMEM((2, nspec, height), f32)] * 2,
            *[pltpu.VMEM((2, 3, nspec, height), f32)] * 2,
            dma(()),
            *[dma((EARLY,))] * 4,
            *[dma((LATE,))] * 4,
            *[dma((10,))] * 2,
        ],
        compiler_params=pltpu.CompilerParams(
            collective_id=0, has_side_effects=True, vmem_limit_bytes=60 * 2**20
        ),
        name="exchange",
    )(
        chemical_fractions,
        spreading_number[None],
        natural_exponent_scale,
        arrhenius_energy,
        incoming_stoichiometry.T,
        outgoing_stoichiometry.T,
    )

    cells = BURN_MAX * height
    updated = pl.pallas_call(
        reaction,
        out_shape=jax.ShapeDtypeStruct((nspec * cx * cy, height), f32),
        in_specs=[hbm] * 5,
        out_specs=vmem,
        scratch_shapes=[
            pltpu.SMEM(ignited_stacks.shape, jnp.int32),
            pltpu.VMEM((cx * cy, height), f32),
            pltpu.VMEM((rows, 4 * room), bf16),
            pltpu.VMEM((2 * pad, rows), bf16),
            dma((5,)),
            pltpu.VMEM((nspec, cells), f32),
            pltpu.VMEM((1, cells), f32),
            pltpu.VMEM((4 * room, cells), bf16),
            pltpu.SMEM((BURN_MAX,), jnp.int32),
        ],
        compiler_params=pltpu.CompilerParams(vmem_limit_bytes=60 * 2**20),
        name="reaction",
    )(
        ignited_stacks,
        mixed.reshape(nspec * cx * cy, height),
        thermal_state.reshape(cx * cy, height),
        logs_mat,
        sums_mat,
    )
    return updated.reshape(shape)


def solution(mesh):
    in_specs = (
        P(None, "wide", "narrow", None),
        P("wide", "narrow", None),
        P("wide", "narrow"),
        P(),
        P(),
        P(),
        P(),
        P(),
    )
    out_specs = P(None, "wide", "narrow", None)
    body = functools.partial(shards, mesh.shape["wide"], mesh.shape["narrow"])
    return jax.shard_map(body, mesh=mesh, in_specs=in_specs, out_specs=out_specs, check_vma=False)
```

```python
import functools

import jax
import jax.numpy as jnp
from jax import lax
from jax.experimental import pallas as pl
from jax.experimental.pallas import tpu as pltpu
from jax.sharding import PartitionSpec as P

BURN_MAX = 8
EARLY = 4
LATE = 4
MESH = pl.DeviceIdType.MESH


def pieces(total, count):
    edges = [total * i // count for i in range(count + 1)]
    return [(lo, hi - lo) for lo, hi in zip(edges[:-1], edges[1:])]


def in_plane(centre, up_edge, down_edge, row, coeff):
    last = centre.shape[1] - 1
    beside = jnp.where(row == 0, up_edge, pltpu.roll(centre, 1, 1))
    beside = beside + jnp.where(row == last, down_edge, pltpu.roll(centre, last, 1))
    beside = beside + pltpu.roll(centre, 1, 2) + pltpu.roll(centre, centre.shape[2] - 1, 2)
    return centre + coeff * (beside - 6.0 * centre)


def rolled(tile):
    return pltpu.roll(tile, 1, 1), pltpu.roll(tile, tile.shape[1] - 1, 1)


def three_parts(values):
    parts = []
    for _ in range(3):
        parts.append(values.astype(jnp.bfloat16).astype(jnp.float32))
        values = values - parts[-1]
    return parts


def rows_by_index(shape, rows):
    index = lax.broadcasted_iota(jnp.int32, shape, 0)
    block = jnp.zeros(shape, jnp.float32)
    for i, row in enumerate(rows):
        block = jnp.where(index == i, row, block)
    return block


def prepare(scale_ref, energy_ref, incoming_ref, outgoing_ref, work, logs_ref, sums_ref):
    nspec, nreact = incoming_ref.shape
    room, pad = logs_ref.shape[1] // 4, sums_ref.shape[0] // 2
    rows = logs_ref.shape[0]
    incoming = incoming_ref[...].astype(jnp.float32)
    work[...] = jnp.zeros_like(work)
    work[0:nspec, 0:nreact] = outgoing_ref[...].astype(jnp.float32)
    work[pad : pad + nspec, 0:nreact] = incoming
    sums_ref[...] = work[0 : 2 * pad, 0:rows].astype(jnp.bfloat16)
    work[...] = jnp.zeros_like(work)
    work[0:nspec, 0:nreact] = incoming
    work[room : room + nspec, 0:nreact] = incoming
    a, e = three_parts(scale_ref[...][None]), three_parts(-energy_ref[...][None])
    extra = (a[0], a[1], a[2], e[0], e[0], e[1], e[1], e[0], e[2])
    work[2 * room : 2 * room + 16, 0:nreact] = rows_by_index((16, nreact), extra)
    logs_ref[...] = work[...].T[0:rows].astype(jnp.bfloat16)


def exchange(
    n_wide, n_narrow, x_ref, coeff_hbm, scale_hbm, energy_hbm, incoming_hbm,
    outgoing_hbm, out_hbm, logs_hbm, sums_hbm, out_ref, logs_ref, sums_ref, store_sem, coeff_ref, scale_ref, energy_ref,
    incoming_ref, outgoing_ref, work, c_ref, load_sem, xv, raw, sums_s, sums_r, part, beyond,
    corner_s, corner_r, touch_s, touch_r, edge_s, edge_r, rest_s, rest_r, local_sem,
    raw_ss, raw_rs, sums_ss, sums_rs, part_ss, part_rs, pass_ss, pass_rs, side_ss, side_rs,
):
    w, n = lax.axis_index("wide"), lax.axis_index("narrow")
    odd = w % 2
    near, far = 1 - odd, odd
    partner = w + 1 - 2 * odd
    other = (w + n_wide + 2 * odd - 1) % n_wide
    target = (w + n_wide + 4 * odd - 2) % n_wide
    source = (w + n_wide + 2 - 4 * odd) % n_wide
    left, right = (n + n_narrow - 1) % n_narrow, (n + 1) % n_narrow
    nspec, _, cy, _ = xv.shape
    early, late = raw.shape[0], part.shape[0]
    early_chunks, late_chunks = pieces(early, EARLY), pieces(late, LATE)

    load = pltpu.make_async_copy(x_ref, xv, local_sem)
    load.start()
    loads = [
        pltpu.make_async_copy(src, dst, load_sem.at[i])
        for i, (src, dst) in enumerate((
            (coeff_hbm, coeff_ref), (scale_hbm, scale_ref), (energy_hbm, energy_ref),
            (incoming_hbm, incoming_ref), (outgoing_hbm, outgoing_ref),
        ))
    ]
    for copy in loads:
        copy.start()
    barrier = pltpu.get_barrier_semaphore()
    greeted = [(w, left), (w, right)]
    greeted += [(a, b) for a in (source, partner) for b in (n, left, right)]
    greeted += [(other, left), (other, right), (target, n)]
    for device in greeted:
        pl.semaphore_signal(barrier, inc=1, device_id=device, device_id_type=MESH)
    load.wait()
    for side, (row, inner) in enumerate(((cy - 1, cy - 2), (0, 1))):
        corner_s[side] = xv[0:early, far, row, :]
        touch_s[side, 0] = xv[early:nspec, near, row, :]
        touch_s[side, 1] = xv[early:nspec, far, row, :]
        edge_s[side] = xv[:, near, row, :]
        rest_s[side, 0] = xv[:, far, row, :]
        rest_s[side, 1] = xv[:, near, inner, :]
        rest_s[side, 2] = xv[:, far, inner, :]
    pl.semaphore_wait(barrier, len(greeted))

    def send(src, dst, ss, rs, device):
        copy = pltpu.make_async_remote_copy(
            src_ref=src, dst_ref=dst, send_sem=ss, recv_sem=rs,
            device_id=device, device_id_type=MESH,
        )
        copy.start()
        return copy

    def sides_of(at, src, dst, row):
        return [
            send(src(side), dst(side), side_ss.at[at + side], side_rs.at[at + side], (row, to))
            for side, to in enumerate((right, left))
        ]

    corners = sides_of(0, lambda i: corner_s.at[i], lambda i: corner_r.at[i], target)
    edges = sides_of(2, lambda i: edge_s.at[i], lambda i: edge_r.at[i], w)
    raws, parts = [], []
    for k in range(max(EARLY, LATE)):
        if k < EARLY:
            sl = pl.ds(*early_chunks[k])
            raws.append(send(xv.at[sl], raw.at[sl], raw_ss.at[k], raw_rs.at[k], (target, n)))
        if k < LATE:
            start, size = late_chunks[k]
            parts.append(
                send(
                    xv.at[pl.ds(early + start, size)], part.at[pl.ds(start, size)],
                    part_ss.at[k], part_rs.at[k], (partner, n),
                )
            )
    rests = sides_of(4, lambda i: rest_s.at[i], lambda i: rest_r.at[i], w)
    touches = sides_of(6, lambda i: touch_s.at[i, 0], lambda i: touch_r.at[i, 0], partner)
    touches += sides_of(8, lambda i: touch_s.at[i, 1], lambda i: touch_r.at[i, 1], other)
    for copy in loads:
        copy.wait()
    for i in range(nspec):
        c_ref[i] = jnp.full(c_ref.shape[1:], coeff_ref[0, i], jnp.float32)
    prepare(scale_ref, energy_ref, incoming_ref, outgoing_ref, work, logs_ref, sums_ref)
    stores = []

    def store(src, dst):
        stores.append(pltpu.make_async_copy(src, dst, store_sem.at[len(stores)]))
        stores[-1].start()

    store(logs_ref, logs_hbm)
    store(sums_ref, sums_hbm)
    for copy in corners + edges:
        copy.wait_recv()

    def rows_of(size):
        return lax.broadcasted_iota(jnp.int32, (size,) + xv.shape[2:], 1)

    sums, passes = [], []
    for k in range(max(EARLY, LATE)):
        if k < LATE:
            sl = pl.ds(*late_chunks[k])
            parts[k].wait_recv()
            passes.append(
                send(part.at[sl], beyond.at[sl], pass_ss.at[k], pass_rs.at[k], (source, n))
            )
        if k < EARLY:
            start, size = early_chunks[k]
            sl, row = pl.ds(start, size), rows_of(size)
            coeff = c_ref[sl]
            square, twice = coeff * coeff, 2.0 * coeff
            own_near, own_far = xv[sl, near], xv[sl, far]
            plane = in_plane(
                own_near, edge_r[0, sl][:, None, :], edge_r[1, sl][:, None, :], row, coeff
            )
            raws[k].wait_recv()
            raw_near, raw_far = raw[sl, far], raw[sl, near]
            sums_s[sl, far] = twice * plane + square * (own_far + raw_near)
            plane = in_plane(
                raw_near, corner_r[0, sl][:, None, :], corner_r[1, sl][:, None, :], row, coeff
            )
            sums_s[sl, near] = twice * plane + square * (own_near + raw_far)
            sums.append(
                send(sums_s.at[sl], sums_r.at[sl], sums_ss.at[k], sums_rs.at[k], (partner, n))
            )

    for copy in rests:
        copy.wait_recv()
    for start, size in pieces(nspec, EARLY + LATE):
        sl, row = pl.ds(start, size), rows_of(size)
        coeff = c_ref[sl]
        square, twice = coeff * coeff, 2.0 * coeff

        def halo(low, high, low_inner, high_inner):
            low, high, low_inner, high_inner = (
                v[:, None, :] for v in (low, high, low_inner, high_inner)
            )
            tile = jnp.where(row == 0, high, high_inner)
            return jnp.where(row == cy - 1, low, jnp.where(row == cy - 2, low_inner, tile))

        own = xv[sl, near], xv[sl, far]
        halos = (
            halo(edge_r[0, sl], edge_r[1, sl], rest_r[0, 1, sl], rest_r[1, 1, sl]),
            halo(rest_r[0, 0, sl], rest_r[1, 0, sl], rest_r[0, 2, sl], rest_r[1, 2, sl]),
        )
        for i, at in enumerate((near, far)):
            mine, side = own[i], halos[i]
            centre = in_plane(mine, *rolled(side), row, coeff) + twice * own[1 - i]
            edge = in_plane(side, *rolled(mine), row, coeff) + twice * halos[1 - i]
            out_ref[sl, at] = in_plane(centre, *rolled(edge), row, coeff) + 2.0 * square * mine

    for copy in touches:
        copy.wait_recv()
    for k in range(max(EARLY, LATE)):
        if k < EARLY:
            sl = pl.ds(*early_chunks[k])
            sums[k].wait_recv()
            out_ref[sl] = out_ref[sl] + sums_r[sl]
            store(out_ref.at[sl], out_hbm.at[sl])
        if k < LATE:
            start, size = late_chunks[k]
            sl, to, row = pl.ds(start, size), pl.ds(early + start, size), rows_of(size)
            coeff = c_ref[to]
            square, twice = coeff * coeff, 2.0 * coeff
            close, second = part[sl, far], part[sl, near]
            plane = twice * in_plane(
                close, touch_r[0, 0, sl][:, None, :], touch_r[1, 0, sl][:, None, :], row, coeff
            )
            passes[k].wait_recv()
            ahead, third = beyond[sl, near], beyond[sl, far]
            out_ref[to, near] = out_ref[to, near] + plane + square * (second + ahead)
            plane = twice * in_plane(
                ahead, touch_r[0, 1, sl][:, None, :], touch_r[1, 1, sl][:, None, :], row, coeff
            )
            out_ref[to, far] = out_ref[to, far] + plane + square * (third + close)
            store(out_ref.at[to], out_hbm.at[to])
    for copy in corners + edges + rests + touches + raws + parts + sums + passes:
        copy.wait_send()
    for copy in stores:
        copy.wait()


def two_parts(values):
    high = values.astype(jnp.bfloat16)
    return high, (values - high.astype(jnp.float32)).astype(jnp.bfloat16)


def reaction(
    marks_hbm, mixed_hbm, heat_hbm, logs_hbm, sums_hbm, out_ref,
    marks_ref, heat_ref, logs_ref, sums_ref, sems, picked, temps, stacked, slots,
):
    loads = [
        pltpu.make_async_copy(src, dst, sems.at[i])
        for i, (src, dst) in enumerate((
            (marks_hbm, marks_ref), (heat_hbm, heat_ref), (mixed_hbm, out_ref),
            (logs_hbm, logs_ref), (sums_hbm, sums_ref),
        ))
    ]
    for copy in loads:
        copy.start()
    nspec = out_ref.shape[0] // heat_ref.shape[0]
    stacks, height = heat_ref.shape
    per_row = marks_ref.shape[1]
    room = stacked.shape[0] // 4
    pad = sums_ref.shape[0] // 2
    stacked[...] = jnp.zeros_like(stacked)
    for k in range(BURN_MAX):
        slots[k] = 0
    loads[0].wait()
    count = jnp.int32(0)
    for i in range(stacks):
        burning = marks_ref[i // per_row, i % per_row]

        @pl.when((burning == 1) & (count < BURN_MAX))
        def _():
            slots[count] = i

        count = count + burning
    for copy in loads[1:]:
        copy.wait()
    for k in range(BURN_MAX):
        cells = pl.ds(k * height, height)
        picked[:, cells] = out_ref[pl.ds(slots[k], nspec, stride=stacks), :]
        temps[:, cells] = heat_ref[pl.ds(slots[k], 1), :]
    t, one = three_parts(1.0 / temps[...]), jnp.ones(temps.shape, jnp.float32)
    extra = (one, one, one, t[0], t[1], t[0], t[1], t[2], t[0])
    extra = rows_by_index((16, temps.shape[1]), extra)
    stacked[2 * room : 2 * room + 16, :] = extra.astype(jnp.bfloat16)
    values = picked[...]
    for substep in range(2):
        high, low = two_parts(jnp.log(values))
        stacked[0:nspec, :] = high
        stacked[room : room + nspec, :] = low
        expo = jnp.dot(logs_ref[...], stacked[...], preferred_element_type=jnp.float32)
        high, low = two_parts(jnp.exp(expo))
        total = jnp.dot(sums_ref[...], high, preferred_element_type=jnp.float32)
        total = total + jnp.dot(sums_ref[...], low, preferred_element_type=jnp.float32)
        gain, loss = total[0:nspec], total[pad : pad + nspec]
        values = values * (values + 0.5 * gain) / (values + 0.5 * loss)
    picked[...] = values
    for k in range(BURN_MAX):

        @pl.when(k < count)
        def _():
            column = picked[:, k * height : (k + 1) * height]
            out_ref[pl.ds(slots[k], nspec, stride=stacks), :] = column


def round_up(value, step):
    return -(-value // step) * step


def shards(
    n_wide,
    n_narrow,
    chemical_fractions,
    thermal_state,
    ignited_stacks,
    spreading_number,
    natural_exponent_scale,
    arrhenius_energy,
    incoming_stoichiometry,
    outgoing_stoichiometry,
):
    shape = chemical_fractions.shape
    nspec, cx, cy, height = shape
    nreact = incoming_stoichiometry.shape[0]
    f32, bf16 = jnp.float32, jnp.bfloat16
    vmem = pl.BlockSpec(memory_space=pltpu.VMEM)
    hbm = pl.BlockSpec(memory_space=pltpu.HBM)
    room, rows = round_up(nspec, 64), round_up(nreact, 16)
    pad, wide = round_up(nspec, 8), round_up(nreact, 128)
    dma = pltpu.SemaphoreType.DMA
    early = nspec // 16 * 8
    mixed, logs_mat, sums_mat = pl.pallas_call(
        functools.partial(exchange, n_wide, n_narrow),
        out_shape=[
            jax.ShapeDtypeStruct(shape, f32),
            jax.ShapeDtypeStruct((rows, 4 * room), bf16),
            jax.ShapeDtypeStruct((2 * pad, rows), bf16),
        ],
        in_specs=[hbm] * 6,
        out_specs=[hbm] * 3,
        scratch_shapes=[
            pltpu.VMEM(shape, f32),
            pltpu.VMEM((rows, 4 * room), bf16),
            pltpu.VMEM((2 * pad, rows), bf16),
            dma((EARLY + LATE + 2,)),
            pltpu.SMEM((1, nspec), f32),
            *[pltpu.VMEM((nreact,), f32)] * 2,
            *[pltpu.VMEM((nspec, nreact), jnp.int32)] * 2,
            pltpu.VMEM((4 * room, wide), f32),
            pltpu.VMEM((nspec, 1, height), f32),
            dma((5,)),
            pltpu.VMEM(shape, f32),
            *[pltpu.VMEM((early,) + shape[1:], f32)] * 3,
            *[pltpu.VMEM((nspec - early,) + shape[1:], f32)] * 2,
            *[pltpu.VMEM((2, early, height), f32)] * 2,
            *[pltpu.VMEM((2, 2, nspec - early, height), f32)] * 2,
            *[pltpu.VMEM((2, nspec, height), f32)] * 2,
            *[pltpu.VMEM((2, 3, nspec, height), f32)] * 2,
            dma(()),
            *[dma((EARLY,))] * 4,
            *[dma((LATE,))] * 4,
            *[dma((10,))] * 2,
        ],
        compiler_params=pltpu.CompilerParams(
            collective_id=0, has_side_effects=True, vmem_limit_bytes=60 * 2**20
        ),
        name="exchange",
    )(
        chemical_fractions,
        spreading_number[None],
        natural_exponent_scale,
        arrhenius_energy,
        incoming_stoichiometry.T,
        outgoing_stoichiometry.T,
    )

    cells = BURN_MAX * height
    updated = pl.pallas_call(
        reaction,
        out_shape=jax.ShapeDtypeStruct((nspec * cx * cy, height), f32),
        in_specs=[hbm] * 5,
        out_specs=vmem,
        scratch_shapes=[
            pltpu.SMEM(ignited_stacks.shape, jnp.int32),
            pltpu.VMEM((cx * cy, height), f32),
            pltpu.VMEM((rows, 4 * room), bf16),
            pltpu.VMEM((2 * pad, rows), bf16),
            dma((5,)),
            pltpu.VMEM((nspec, cells), f32),
            pltpu.VMEM((1, cells), f32),
            pltpu.VMEM((4 * room, cells), bf16),
            pltpu.SMEM((BURN_MAX,), jnp.int32),
        ],
        compiler_params=pltpu.CompilerParams(vmem_limit_bytes=60 * 2**20),
        name="reaction",
    )(
        ignited_stacks,
        mixed.reshape(nspec * cx * cy, height),
        thermal_state.reshape(cx * cy, height),
        logs_mat,
        sums_mat,
    )
    return updated.reshape(shape)


def solution(mesh):
    in_specs = (
        P(None, "wide", "narrow", None),
        P("wide", "narrow", None),
        P("wide", "narrow"),
        P(),
        P(),
        P(),
        P(),
        P(),
    )
    out_specs = P(None, "wide", "narrow", None)
    body = functools.partial(shards, mesh.shape["wide"], mesh.shape["narrow"])
    return jax.shard_map(body, mesh=mesh, in_specs=in_specs, out_specs=out_specs, check_vma=False)
```
